32 devices in a mesh: dp: 4 (over y, x), fsdp: 8 (over z, core).
Axes of the slice: x: 2, y: 2, z: 4, core: 2. Of those that a mesh axis runs over, the one named last changes fastest.
Arguments:
- mlp_input: bfloat16 [256, 4096], P('dp', 'fsdp'), may hold values from -6 to 6
- residual_in: bfloat16 [256, 4096], P(('dp', 'fsdp')), may hold values from -6 to 6
- gate_weight: bfloat16 [4096, 14336], P(None, 'fsdp'), may hold values from -0.09375 to 0.09375
- up_weight: bfloat16 [4096, 14336], P(None, 'fsdp'), may hold values from -0.09375 to 0.09375
- down_weight: bfloat16 [14336, 4096], P('fsdp'), may hold values from -0.046875 to 0.046875
- span_index: bfloat16 [16384, 4096], P(('dp', 'fsdp')), may hold values from -6 to 6
- positive_keys: bfloat16 [256, 4096], P(('dp', 'fsdp')), may hold values from -6 to 6
- request_rows: int32 [32, 32, 32], P(None, ('dp', 'fsdp')), may hold values from 0 to 511, as said below
- request_counts: int32 [32, 32], P(None, ('dp', 'fsdp')), may hold values from 0 to 32, as said below
- negative_slots: int32 [256, 64], P(('dp', 'fsdp')), may hold values from 0 to 1023, as said below
Outputs:
- query_loss: float32 [256], P(('dp', 'fsdp'))
- input_grad: bfloat16 [256, 4096], P('dp', 'fsdp')
- gate_grad: bfloat16 [4096, 14336], P('dp', 'fsdp')
- up_grad: bfloat16 [4096, 14336], P('dp', 'fsdp')
- down_grad: bfloat16 [14336, 4096], P('fsdp', 'dp')
The draws below stay inside these ranges and needn't reach their ends.
Inputs may be any that keep to these rules, and one draw needn't show every extreme that they name: `request_rows`: entry [r, o, s] is a local row of shard o; it is read only where s < request_counts[r, o]. `request_counts`: for each requesting device r the counts over the 32 shards sum to 512, and some shard gets exactly 32. `negative_slots`: rows q of device r = q // 8; an entry o * 32 + s names slot s of shard o with s < request_counts[r, o]; the 512 entries of a device use each such slot exactly once.
All inputs are finite; a program needn't handle non-finite values.
Results may differ from the reference program's by a relative error of at most 0.017.
Values may be sent and summed in bfloat16 or wider, within the bound.
No kernel may reach another device: no remote copies, remote signals or barrier semaphores. Data moves between devices by JAX's collectives and lax.ppermute only.
A program may use at most 192 MiB of HBM per device.

```python
import jax
import jax.numpy as jnp
from jax import lax

D = 4096
FF = 14336
NEG = 64
QD = 8
CH_DEV = 512
OWNERS = 32
QUERIES = 256
CAP = 32
SPANS = 16384
N_DP = 4


def request_plan(key):
    half_cap = QD * NEG // OWNERS
    slot_cap = 2 * half_cap

    def plan_one(sub_key):
        key_order, key_lift, key_rank = jax.random.split(sub_key, 3)
        middle = (jax.random.permutation(key_order, OWNERS - 2) + 1).astype(jnp.int32)
        owner_order = jnp.concatenate([jnp.array([OWNERS - 1], jnp.int32), middle[:1], jnp.array([0], jnp.int32), middle[1:]])
        count_lift = jax.random.randint(key_lift, (OWNERS // 2,), 0, half_cap + 1)
        count_lift = count_lift.at[0].set(half_cap)
        pattern = jnp.stack([half_cap + count_lift, half_cap - count_lift], axis=1).reshape(-1).astype(jnp.int32)
        counts = jnp.zeros((OWNERS,), jnp.int32).at[owner_order].set(pattern)
        places = jnp.arange(OWNERS * slot_cap, dtype=jnp.int32)
        live_mask = places % slot_cap < counts[places // slot_cap]
        slot_rank = jax.random.permutation(key_rank, OWNERS * slot_cap).astype(jnp.int32)
        sort_key = jnp.where(live_mask, slot_rank, slot_rank + OWNERS * slot_cap)
        chosen = jnp.argsort(sort_key, stable=True)[:QD * NEG].astype(jnp.int32)
        return (counts, chosen.reshape(QD, NEG))
    device_keys = jax.random.split(jax.random.fold_in(key, 7), OWNERS)
    return jax.vmap(plan_one)(device_keys)


def draw_request_counts(key, part):
    counts, chosen = request_plan(key)
    return counts


def draw_negative_slots(key, part):
    counts, chosen = request_plan(key)
    return chosen.reshape(OWNERS * QD, NEG)


def draw_request_rows(key, part):
    return jax.random.randint(jax.random.fold_in(key, 11), (OWNERS, OWNERS, CAP), 0, CH_DEV).astype(jnp.int32)


def block_scale(key, shape, pieces, least, high):
    gain = 1.0
    for position, blocks in pieces:
        draws = jax.random.uniform(jax.random.fold_in(jax.random.fold_in(key, 6), position), (blocks,), jnp.float32, least / len(pieces), high / len(pieces))
        gain = gain * jnp.repeat(jnp.exp(draws), shape[position] // blocks).reshape((-1,) + (1,) * (len(shape) - 1 - position))
    return gain


def centred(stream_key, extent, width, bound, pieces=(), kind=jnp.bfloat16):
    level = block_scale(stream_key, extent, pieces, -0.22, 0.18) if pieces else 1.0
    values = jax.random.normal(stream_key, extent, jnp.float32) * width * level
    return jnp.minimum(jnp.maximum(values, -bound), bound).astype(kind)


def setup_inputs(seed: int = 0) -> dict:
    seeds = jax.random.split(jax.random.key(seed), 11)
    mlp_input = centred(seeds[0], (QUERIES, D), 1.0, 6.0, ((0, 4), (1, 8)))
    residual_in = centred(seeds[1], (QUERIES, D), 1.0, 6.0, ((0, 32),))
    gate_weight = centred(seeds[2], (D, FF), D ** -0.5, 0.09375, ((1, 8),))
    up_weight = centred(seeds[3], (D, FF), D ** -0.5, 0.09375, ((1, 8),))
    down_weight = centred(seeds[4], (FF, D), FF ** -0.5, 0.046875, ((0, 8),))
    span_index = centred(seeds[5], (SPANS, D), 1.0, 6.0, ((0, 32),))
    positive_keys = centred(seeds[6], (QUERIES, D), 1.0, 6.0, ((0, 32),))
    request_rows = draw_request_rows(jax.random.fold_in(seeds[10], 71), 0)
    request_counts = draw_request_counts(jax.random.fold_in(seeds[10], 71), 0)
    negative_slots = draw_negative_slots(jax.random.fold_in(seeds[10], 71), 0)
    return dict(mlp_input=mlp_input, residual_in=residual_in, gate_weight=gate_weight, up_weight=up_weight, down_weight=down_weight, span_index=span_index, positive_keys=positive_keys, request_rows=request_rows, request_counts=request_counts, negative_slots=negative_slots)


inverse_temp = 50.0
eps = 1e-06

def silu_grad(gate_act):
    sigmoid_gate = jax.nn.sigmoid(gate_act)
    return sigmoid_gate * (1.0 + gate_act * (1.0 - sigmoid_gate))

def contrast(unit_rows, row_norm, key_block):
    key_unit = key_block / jnp.sqrt(lax.optimization_barrier(jnp.sum(key_block * key_block, axis=-1, keepdims=True)) + eps)
    scores = inverse_temp * jnp.einsum('qd,qnd->qn', unit_rows, key_unit, precision=lax.Precision.HIGHEST)
    weights = jnp.exp(scores)
    exp_total = lax.optimization_barrier(jnp.sum(weights, axis=-1))
    query_loss = jnp.log(exp_total) - scores[:, 0]
    column = lax.broadcasted_iota(jnp.int32, scores.shape, 1)
    coeffs = weights / exp_total[:, None] - (column == 0).astype(scores.dtype)
    pull_term = inverse_temp * jnp.einsum('qn,qnd->qd', coeffs, key_unit, precision=lax.Precision.HIGHEST)
    inner_term = lax.optimization_barrier(jnp.sum(coeffs * scores, axis=-1))
    head_grad = ((pull_term - inner_term[:, None] * unit_rows) / row_norm[:, None]).astype(jnp.bfloat16)
    return (query_loss, head_grad)

def group_sum(left_rows, right_rows, groups):
    group_rows = left_rows.shape[0] // groups
    result = jnp.zeros((left_rows.shape[1], right_rows.shape[1]), jnp.float32)
    for group_index in range(groups):
        lower = group_index * group_rows
        partial_term = lax.dot_general(left_rows[lower:lower + group_rows], right_rows[lower:lower + group_rows], (((0,), (0,)), ((), ())), preferred_element_type=jnp.float32)
        rounded = lax.optimization_barrier(partial_term.astype(jnp.bfloat16))
        result = result + rounded.astype(jnp.float32)
    return result.astype(jnp.bfloat16)

def reference(mlp_input, residual_in, gate_weight, up_weight, down_weight, span_index, positive_keys, request_rows, request_counts, negative_slots):
    gate_act = jnp.dot(mlp_input, gate_weight, preferred_element_type=jnp.float32)
    up_act = jnp.dot(mlp_input, up_weight, preferred_element_type=jnp.float32)
    hidden = (jax.nn.silu(gate_act) * up_act).astype(jnp.bfloat16)
    top_state = jnp.dot(hidden, down_weight, preferred_element_type=jnp.float32) + residual_in.astype(jnp.float32)
    row_norm = jnp.sqrt(lax.optimization_barrier(jnp.sum(top_state * top_state, axis=-1)) + eps)
    unit_rows = top_state / row_norm[:, None]

    def per_device(block_args):
        unit_block, norm_block, positive_block, slot_block, row_table, count_table = block_args
        owner_of = slot_block // CAP
        place_of = slot_block % CAP
        local_row = row_table[owner_of, place_of]
        live_mask = place_of < count_table[owner_of]
        fetched = jnp.take(span_index, (owner_of * CH_DEV + local_row).astype(jnp.int32), axis=0).astype(jnp.float32)
        fetched = jnp.where(live_mask[..., None], fetched, jnp.zeros_like(fetched))
        key_block = jnp.concatenate([positive_block.astype(jnp.float32)[:, None, :], fetched], axis=1)
        return contrast(unit_block, norm_block, key_block)
    query_loss, head_grad = lax.map(per_device, (unit_rows.reshape(OWNERS, QD, D), row_norm.reshape(OWNERS, QD), positive_keys.reshape(OWNERS, QD, D), negative_slots.reshape(OWNERS, QD, NEG), request_rows, request_counts))
    query_loss = query_loss.reshape(-1)
    head_grad = head_grad.reshape(-1, D)
    hidden_grad = jnp.dot(head_grad, down_weight.T, preferred_element_type=jnp.float32)
    gate_grad_act = (hidden_grad * up_act * silu_grad(gate_act)).astype(jnp.bfloat16)
    up_grad_act = (hidden_grad * jax.nn.silu(gate_act)).astype(jnp.bfloat16)
    input_grad = (jnp.dot(gate_grad_act, gate_weight.T, preferred_element_type=jnp.float32) + jnp.dot(up_grad_act, up_weight.T, preferred_element_type=jnp.float32)).astype(jnp.bfloat16)
    gate_grad = group_sum(mlp_input, gate_grad_act, N_DP)
    up_grad = group_sum(mlp_input, up_grad_act, N_DP)
    down_grad = group_sum(hidden, head_grad, N_DP)
    return (query_loss, input_grad, gate_grad, up_grad, down_grad)
```

```python
import jax
import jax.numpy as jnp
from jax import lax
from jax.sharding import PartitionSpec as P

inverse_temp = 50.0
eps = 1e-06
contract_first = (((0,), (0,)), ((), ()))
contract_last = (((1,), (1,)), ((), ()))
every = ("dp", "fsdp")


def silu_grad(gate_act):
    sigmoid_gate = jax.nn.sigmoid(gate_act)
    return sigmoid_gate * (1.0 + gate_act * (1.0 - sigmoid_gate))


def dot32(left, right, dims=(((1,), (0,)), ((), ()))):
    return lax.dot_general(left, right, dims, preferred_element_type=jnp.float32)


def norm_of(rows):
    return jnp.sqrt(jnp.sum(rows * rows, axis=-1) + eps)


def sum_to_owner(partial, axis, parts):
    pieces = lax.all_to_all(partial, axis, split_axis=0, concat_axis=0, tiled=True)
    pieces = pieces.reshape(parts, partial.shape[0] // parts, partial.shape[1])
    return jnp.sum(pieces.astype(jnp.float32), axis=0)


def use_counts(all_slots, row_table, count_table, me, shard_rows):
    owners, slot_cap = row_table.shape
    queries = all_slots.shape[0]
    slot = lax.broadcasted_iota(jnp.int32, (1, 1, slot_cap), 2) + me * slot_cap
    asked = jnp.sum((all_slots[:, :, None] == slot).astype(jnp.float32), axis=1)
    asked = asked.reshape(owners, queries // owners, slot_cap)
    live = lax.broadcasted_iota(jnp.int32, (owners, 1, slot_cap), 2) < count_table[:, None, None]
    used = jnp.where(live, asked, 0.0)
    dead = jnp.sum(asked - used, axis=-1).reshape(queries)
    row = lax.broadcasted_iota(jnp.int32, (1, 1, shard_rows), 2)
    picks = (row_table[:, :, None] == row).astype(jnp.bfloat16)
    counts = lax.dot_general(
        used.astype(jnp.bfloat16),
        picks,
        (((2,), (1,)), ((0,), (0,))),
        preferred_element_type=jnp.float32,
    )
    return counts.reshape(queries, shard_rows), dead


def shards(
    mlp_input,
    residual_in,
    gate_weight,
    up_weight,
    down_weight,
    span_index,
    positive_keys,
    request_rows,
    request_counts,
    negative_slots,
):
    dp_count = lax.axis_size("dp")
    fsdp_count = lax.axis_size("fsdp")
    owners = dp_count * fsdp_count
    me = lax.axis_index(every)
    width = span_index.shape[1]

    whole_input = lax.all_gather(mlp_input, "fsdp", axis=1, tiled=True)
    gate_act = dot32(whole_input, gate_weight)
    up_act = dot32(whole_input, up_weight)
    hidden = (jax.nn.silu(gate_act) * up_act).astype(jnp.bfloat16)
    branch = sum_to_owner(dot32(hidden, down_weight).astype(jnp.bfloat16), "fsdp", fsdp_count)
    top_state = branch + residual_in.astype(jnp.float32)
    row_norm = norm_of(top_state)
    unit_rows = top_state / row_norm[:, None]

    all_slots = lax.all_gather(negative_slots, every, axis=0, tiled=True)
    counts, dead = use_counts(
        all_slots, request_rows[:, 0, :], request_counts[:, 0], me, span_index.shape[0]
    )
    span_values = span_index.astype(jnp.float32)
    span_norm = norm_of(span_values)
    all_states = lax.all_gather(top_state.astype(jnp.bfloat16), "fsdp", axis=0, tiled=True)
    all_states = lax.all_gather(all_states, "dp", axis=0, tiled=True)
    state_norm = norm_of(all_states.astype(jnp.float32))
    raw_scores = dot32(all_states, span_index, contract_last)
    scores = inverse_temp * raw_scores / state_norm[:, None] / span_norm[None, :]
    weights = counts * jnp.exp(scores)
    shard_total = jnp.sum(weights, axis=-1) + dead
    shard_pull = dot32((weights / span_norm[None, :]).astype(jnp.bfloat16), span_index)

    total_high = shard_total.astype(jnp.bfloat16)
    total_low = (shard_total - total_high.astype(jnp.float32)).astype(jnp.bfloat16)
    column = lax.broadcasted_iota(jnp.int32, (shard_total.shape[0], 128), 1)
    totals = jnp.where(column == 0, total_high[:, None], jnp.where(column == 1, total_low[:, None], 0))
    sums = sum_to_owner(
        jnp.concatenate([shard_pull.astype(jnp.bfloat16), totals.astype(jnp.bfloat16)], axis=1),
        every,
        owners,
    )
    negative_total = sums[:, width] + sums[:, width + 1]
    positive_rows = positive_keys.astype(jnp.float32)
    positive_unit = positive_rows / norm_of(positive_rows)[:, None]
    positive_score = inverse_temp * jnp.sum(unit_rows * positive_unit, axis=-1)
    exp_total = jnp.exp(positive_score) + negative_total
    query_loss = jnp.log(exp_total) - positive_score
    pull = (sums[:, :width] - negative_total[:, None] * positive_unit) / exp_total[:, None]
    inner = jnp.sum(pull * unit_rows, axis=-1)
    head_grad = (
        inverse_temp * (pull - inner[:, None] * unit_rows) / row_norm[:, None]
    ).astype(jnp.bfloat16)

    gathered_grad = lax.all_gather(head_grad, "fsdp", axis=0, tiled=True)
    hidden_grad = dot32(gathered_grad, down_weight, contract_last)
    gate_grad_act = (hidden_grad * up_act * silu_grad(gate_act)).astype(jnp.bfloat16)
    up_grad_act = (hidden_grad * jax.nn.silu(gate_act)).astype(jnp.bfloat16)
    input_term = dot32(gate_grad_act, gate_weight, contract_last) + dot32(
        up_grad_act, up_weight, contract_last
    )
    input_grad = lax.psum_scatter(
        input_term.astype(jnp.bfloat16), "fsdp", scatter_dimension=1, tiled=True
    )

    def columns_of_all(rows):
        return lax.all_to_all(rows, "dp", split_axis=1, concat_axis=0, tiled=True)

    def rows_of_all(rows):
        return lax.all_gather(rows, "dp", axis=0, tiled=True)

    input_columns = columns_of_all(whole_input)
    grad_columns = columns_of_all(gathered_grad)
    down_grad = dot32(rows_of_all(hidden), grad_columns, contract_first).astype(jnp.bfloat16)
    gate_grad = dot32(input_columns, rows_of_all(gate_grad_act), contract_first).astype(jnp.bfloat16)
    up_grad = dot32(input_columns, rows_of_all(up_grad_act), contract_first).astype(jnp.bfloat16)
    return (query_loss, input_grad, gate_grad, up_grad, down_grad)


def solution(mesh):
    return jax.shard_map(
        shards,
        mesh=mesh,
        in_specs=(
            P("dp", "fsdp"),
            P(("dp", "fsdp"), None),
            P(None, "fsdp"),
            P(None, "fsdp"),
            P("fsdp", None),
            P(("dp", "fsdp"), None),
            P(("dp", "fsdp"), None),
            P(None, ("dp", "fsdp"), None),
            P(None, ("dp", "fsdp")),
            P(("dp", "fsdp"), None),
        ),
        out_specs=(
            P(("dp", "fsdp")),
            P("dp", "fsdp"),
            P("dp", "fsdp"),
            P("dp", "fsdp"),
            P("fsdp", "dp"),
        ),
        check_vma=False,
    )
```

```python
import jax
import jax.numpy as jnp
from jax import lax
from jax.sharding import PartitionSpec as P

inverse_temp = 50.0
eps = 1e-06
contract_first = (((0,), (0,)), ((), ()))
contract_last = (((1,), (1,)), ((), ()))
every = ("dp", "fsdp")


def silu_grad(gate_act):
    sigmoid_gate = jax.nn.sigmoid(gate_act)
    return sigmoid_gate * (1.0 + gate_act * (1.0 - sigmoid_gate))


def dot32(left, right, dims=(((1,), (0,)), ((), ()))):
    return lax.dot_general(left, right, dims, preferred_element_type=jnp.float32)


def norm_of(rows):
    return jnp.sqrt(jnp.sum(rows * rows, axis=-1) + eps)


def swap(x, axis, difference):
    pairs = [(i, i ^ difference) for i in range(lax.axis_size(axis))]
    return lax.ppermute(x, axis, pairs)


def swap_core(x):
    return swap(x, "fsdp", 1)


def gather_chips(x):
    chips = lax.axis_size("fsdp") // 2
    return jnp.concatenate([x] + [swap(x, "fsdp", 2 * j) for j in range(1, chips)], axis=0)


def gather_dp(x):
    return jnp.concatenate([x] + [swap(x, "dp", j) for j in range(1, lax.axis_size("dp"))], axis=0)


def gather_core(x):
    return jnp.concatenate([x, swap_core(x)], axis=0)


def add_up(pieces):
    total = pieces[0].astype(jnp.float32)
    for piece in pieces[1:]:
        total = total + piece.astype(jnp.float32)
    return total


def sum_core(x):
    rows = x.shape[0] // 2
    return add_up([x[:rows], swap_core(x[rows:])])


def sum_over(x, axis, parts, unit):
    rows = x.shape[0] // parts
    return add_up(
        [x[:rows]]
        + [swap(x[j * rows : (j + 1) * rows], axis, j * unit) for j in range(1, parts)]
    )


def sum_chips(x):
    return sum_over(x, "fsdp", lax.axis_size("fsdp") // 2, 2)


def sum_dp(x):
    return sum_over(x, "dp", lax.axis_size("dp"), 1)


def relative_order(blocks, block_rows):
    mine = lax.axis_index("fsdp")
    rows = blocks * block_rows
    place = lax.broadcasted_iota(jnp.int32, (rows, rows), 0)
    block, row = place // block_rows, place % block_rows
    core, chip = block // (blocks // 2), block % (blocks // 2)
    source = jnp.bitwise_xor(mine, 2 * chip + core) * block_rows + row
    return (source == lax.broadcasted_iota(jnp.int32, (rows, rows), 1)).astype(jnp.bfloat16)


def in_fsdp_order(pieces):
    mine = lax.axis_index("fsdp")
    blocks = pieces.shape[0]
    pieces = pieces.reshape((2, blocks // 2) + pieces.shape[1:])
    pieces = jnp.where(mine % 2 == 1, pieces[::-1], pieces)
    bit = 1
    while bit < blocks // 2:
        split = pieces.reshape((2, blocks // 4 // bit, 2, bit) + pieces.shape[2:])
        split = jnp.where((mine // (2 * bit)) % 2 == 1, split[:, :, ::-1], split)
        pieces = split.reshape(pieces.shape)
        bit *= 2
    return jnp.swapaxes(pieces, 0, 1).reshape((blocks,) + pieces.shape[2:])


def use_counts(slots, row_table, count_table, shard, shard_rows):
    devices, queries, negatives = slots.shape
    slot_cap = row_table.shape[1]
    slot = lax.broadcasted_iota(jnp.int32, (1, 1, 1, slot_cap), 3) + shard * slot_cap
    asked = jnp.sum((slots[..., None] == slot).astype(jnp.float32), axis=2)
    live = lax.broadcasted_iota(jnp.int32, (devices, 1, slot_cap), 2) < count_table[:, None, None]
    used = jnp.where(live, asked, 0.0)
    dead = jnp.sum(asked - used, axis=-1).reshape(devices * queries)
    row = lax.broadcasted_iota(jnp.int32, (1, 1, shard_rows), 2)
    picks = (row_table[:, :, None] == row).astype(jnp.bfloat16)
    counts = lax.dot_general(
        used.astype(jnp.bfloat16),
        picks,
        (((2,), (1,)), ((0,), (0,))),
        preferred_element_type=jnp.float32,
    )
    return counts.reshape(devices * queries, shard_rows), dead


def shards(
    mlp_input,
    residual_in,
    gate_weight,
    up_weight,
    down_weight,
    span_index,
    positive_keys,
    request_rows,
    request_counts,
    negative_slots,
):
    dp_count = lax.axis_size("dp")
    fsdp_count = lax.axis_size("fsdp")
    chips = fsdp_count // 2
    my_dp, my_fsdp = lax.axis_index("dp"), lax.axis_index("fsdp")
    me = my_dp * fsdp_count + my_fsdp
    width = span_index.shape[1]
    own_queries = negative_slots.shape[0]
    group_rows = mlp_input.shape[0]

    pieces = gather_core(gather_chips(mlp_input[None]))
    whole_input = jnp.swapaxes(in_fsdp_order(pieces), 0, 1).reshape(group_rows, width)
    to_relative = relative_order(fsdp_count, own_queries)
    whole_input = dot32(to_relative, whole_input).astype(jnp.bfloat16)

    chip_index = gather_core(span_index[None])
    tables = gather_core(jnp.concatenate([request_rows[:, 0, :], request_counts], axis=1)[None])
    slots = gather_dp(gather_chips(negative_slots[None]))
    j = jnp.arange(dp_count * chips, dtype=jnp.int32)
    asker = jnp.bitwise_xor(my_dp, j // chips) * fsdp_count + jnp.bitwise_xor(
        my_fsdp, 2 * (j % chips)
    )
    tables = jnp.take(tables, asker, axis=1)
    counts, dead = [], 0.0
    for k in range(2):
        shard_counts, shard_dead = use_counts(
            slots,
            tables[k, :, :-1],
            tables[k, :, -1],
            jnp.bitwise_xor(me, k),
            span_index.shape[0],
        )
        counts.append(shard_counts)
        dead = dead + shard_dead
    counts = jnp.concatenate(counts, axis=1)
    chip_index = chip_index.reshape(-1, width)
    index_norm = norm_of(chip_index.astype(jnp.float32))

    gate_act = dot32(whole_input, gate_weight)
    up_act = dot32(whole_input, up_weight)
    hidden = (jax.nn.silu(gate_act) * up_act).astype(jnp.bfloat16)
    branch = sum_core(dot32(hidden, down_weight).astype(jnp.bfloat16))
    branch = sum_chips(branch.astype(jnp.bfloat16))
    top_state = branch + residual_in.astype(jnp.float32)
    row_norm = norm_of(top_state)
    unit_rows = top_state / row_norm[:, None]

    states = gather_dp(gather_chips(top_state.astype(jnp.bfloat16)))
    state_norm = norm_of(states.astype(jnp.float32))
    raw_scores = dot32(states, chip_index, contract_last)
    scores = inverse_temp * raw_scores / state_norm[:, None] / index_norm[None, :]
    weights = counts * jnp.exp(scores)
    chip_total = jnp.sum(weights, axis=-1) + dead
    chip_pull = dot32((weights / index_norm[None, :]).astype(jnp.bfloat16), chip_index)

    column = lax.broadcasted_iota(jnp.int32, (chip_total.shape[0], 128), 1)
    totals = jnp.where(column == 0, chip_total[:, None], 0.0).astype(jnp.bfloat16)
    sums = sum_dp(jnp.concatenate([chip_pull.astype(jnp.bfloat16), totals], axis=1))
    sums = sum_chips(sums.astype(jnp.bfloat16))
    negative_total = sums[:, width]
    positive_rows = positive_keys.astype(jnp.float32)
    positive_unit = positive_rows / norm_of(positive_rows)[:, None]
    positive_score = inverse_temp * jnp.sum(unit_rows * positive_unit, axis=-1)
    exp_total = jnp.exp(positive_score) + negative_total
    query_loss = jnp.log(exp_total) - positive_score
    pull = (sums[:, :width] - negative_total[:, None] * positive_unit) / exp_total[:, None]
    inner = jnp.sum(pull * unit_rows, axis=-1)
    head_grad = (
        inverse_temp * (pull - inner[:, None] * unit_rows) / row_norm[:, None]
    ).astype(jnp.bfloat16)

    def columns_of_all(rows):
        part = rows.shape[1] // dp_count
        return jnp.concatenate(
            [
                swap(
                    lax.dynamic_slice_in_dim(rows, jnp.bitwise_xor(my_dp, k) * part, part, axis=1),
                    "dp",
                    k,
                )
                if k
                else lax.dynamic_slice_in_dim(rows, my_dp * part, part, axis=1)
                for k in range(dp_count)
            ],
            axis=0,
        )

    input_columns = columns_of_all(whole_input)
    gate_all = gather_dp(gate_act.astype(jnp.bfloat16)).astype(jnp.float32)
    up_all = gather_dp(up_act.astype(jnp.bfloat16)).astype(jnp.float32)

    gathered_grad = gather_core(gather_chips(head_grad))
    hidden_grad = dot32(gathered_grad, down_weight, contract_last)
    own_gate_grad = (hidden_grad * up_act * silu_grad(gate_act)).astype(jnp.bfloat16)
    own_up_grad = (hidden_grad * jax.nn.silu(gate_act)).astype(jnp.bfloat16)
    own_gate_grad = dot32(to_relative, own_gate_grad, contract_first).astype(jnp.bfloat16)
    own_up_grad = dot32(to_relative, own_up_grad, contract_first).astype(jnp.bfloat16)
    input_term = dot32(own_gate_grad, gate_weight, contract_last) + dot32(
        own_up_grad, up_weight, contract_last
    )
    input_blocks = input_term.astype(jnp.bfloat16).reshape(group_rows, fsdp_count, -1)
    source = jnp.arange(fsdp_count, dtype=jnp.int32)
    source = jnp.bitwise_xor(my_fsdp, 2 * (source % chips) + source // chips)
    input_blocks = jnp.take(jnp.swapaxes(input_blocks, 0, 1), source, axis=0)
    input_grad = sum_chips(sum_core(input_blocks).astype(jnp.bfloat16))[0].astype(jnp.bfloat16)

    grad_columns = columns_of_all(gathered_grad)
    hidden_all = (jax.nn.silu(gate_all) * up_all).astype(jnp.bfloat16)
    down_grad = dot32(hidden_all, grad_columns, contract_first).astype(jnp.bfloat16)
    grad_all = gather_dp(hidden_grad.astype(jnp.bfloat16)).astype(jnp.float32)
    gate_grad_all = (grad_all * up_all * silu_grad(gate_all)).astype(jnp.bfloat16)
    up_grad_all = (grad_all * jax.nn.silu(gate_all)).astype(jnp.bfloat16)
    gate_grad = dot32(input_columns.T, gate_grad_all).astype(jnp.bfloat16)
    up_grad = dot32(input_columns.T, up_grad_all).astype(jnp.bfloat16)
    return (query_loss, input_grad, gate_grad, up_grad, down_grad)


def solution(mesh):
    return jax.shard_map(
        shards,
        mesh=mesh,
        in_specs=(
            P("dp", "fsdp"),
            P(("dp", "fsdp"), None),
            P(None, "fsdp"),
            P(None, "fsdp"),
            P("fsdp", None),
            P(("dp", "fsdp"), None),
            P(("dp", "fsdp"), None),
            P(None, ("dp", "fsdp"), None),
            P(None, ("dp", "fsdp")),
            P(("dp", "fsdp"), None),
        ),
        out_specs=(
            P(("dp", "fsdp")),
            P("dp", "fsdp"),
            P("dp", "fsdp"),
            P("dp", "fsdp"),
            P("fsdp", "dp"),
        ),
        check_vma=False,
    )
```

```python
import jax
import jax.numpy as jnp
from jax import lax
from jax.experimental import pallas as pl
from jax.experimental.pallas import tpu as pltpu
from jax.sharding import PartitionSpec as P

inverse_temp = 50.0
eps = 1e-06
contract_first = (((0,), (0,)), ((), ()))
contract_last = (((1,), (1,)), ((), ()))
every = ("dp", "fsdp")


def sigmoid(v):
    return 1.0 / (1.0 + jnp.exp(-v))


def activation_grads(hidden_grad, gate_act, up_act):
    gate = sigmoid(gate_act)
    gate_grad = hidden_grad * up_act * gate * (1.0 + gate_act * (1.0 - gate))
    return gate_grad.astype(jnp.bfloat16), (hidden_grad * gate_act * gate).astype(jnp.bfloat16)


def dot32(left, right, dims=(((1,), (0,)), ((), ()))):
    return lax.dot_general(left, right, dims, preferred_element_type=jnp.float32)


def norm_of(rows):
    return jnp.sqrt(jnp.sum(rows * rows, axis=-1) + eps)


def swap(x, axis, difference):
    pairs = [(i, i ^ difference) for i in range(lax.axis_size(axis))]
    return lax.ppermute(x, axis, pairs)


def swap_core(x):
    return swap(x, "fsdp", 1)


def gather_chips(x):
    chips = lax.axis_size("fsdp") // 2
    return jnp.concatenate([x] + [swap(x, "fsdp", 2 * j) for j in range(1, chips)], axis=0)


def gather_dp(x):
    return jnp.concatenate([x] + [swap(x, "dp", j) for j in range(1, lax.axis_size("dp"))], axis=0)


def gather_core(x):
    return jnp.concatenate([x, swap_core(x)], axis=0)


def add_up(pieces):
    total = pieces[0].astype(jnp.float32)
    for piece in pieces[1:]:
        total = total + piece.astype(jnp.float32)
    return total


def sum_core(x):
    rows = x.shape[0] // 2
    return add_up([x[:rows], swap_core(x[rows:])])


def sum_over(x, axis, parts, unit):
    rows = x.shape[0] // parts
    return add_up(
        [x[:rows]]
        + [swap(x[j * rows : (j + 1) * rows], axis, j * unit) for j in range(1, parts)]
    )


def sum_chips(x):
    return sum_over(x, "fsdp", lax.axis_size("fsdp") // 2, 2)


def sum_dp(x):
    return sum_over(x, "dp", lax.axis_size("dp"), 1)


def relative_order(mine, blocks, block_rows):
    rows = blocks * block_rows
    place = lax.broadcasted_iota(jnp.int32, (rows, rows), 0)
    block, row = place // block_rows, place % block_rows
    core, chip = block // (blocks // 2), block % (blocks // 2)
    source = jnp.bitwise_xor(mine[:, None], 2 * chip + core) * block_rows + row
    return (source == lax.broadcasted_iota(jnp.int32, (rows, rows), 1)).astype(jnp.bfloat16)


def use_counts(slots, row_table, count_table, shard, shard_rows):
    devices, queries, negatives = slots.shape
    slot_cap = row_table.shape[1]
    slot = lax.broadcasted_iota(jnp.int32, (1, 1, 1, slot_cap), 3) + shard[:, None, None, None] * slot_cap
    asked = jnp.sum((slots[..., None] == slot).astype(jnp.float32), axis=2)
    live = lax.broadcasted_iota(jnp.int32, (devices, 1, slot_cap), 2) < count_table[:, None, None]
    used = jnp.where(live, asked, 0.0)
    dead = jnp.sum(asked - used, axis=-1).reshape(devices * queries)
    row = lax.broadcasted_iota(jnp.int32, (1, 1, shard_rows), 2)
    picks = (row_table[:, :, None] == row).astype(jnp.bfloat16)
    counts = lax.dot_general(
        used.astype(jnp.bfloat16),
        picks,
        (((2,), (1,)), ((0,), (0,))),
        preferred_element_type=jnp.float32,
    )
    return counts.reshape(devices * queries, shard_rows), dead


in_vmem = pl.BlockSpec(memory_space=pltpu.VMEM)
in_smem = pl.BlockSpec(memory_space=pltpu.SMEM)
in_hbm = pl.BlockSpec(memory_space=pltpu.HBM)
mib = 2**20


def held(x):
    return pltpu.with_memory_space_constraint(x, pltpu.VMEM)


def in_place(x):
    return pltpu.with_memory_space_constraint(x, pltpu.HBM)


def shape_of(shape, dtype=jnp.bfloat16):
    return jax.ShapeDtypeStruct(shape, dtype)


def kernel_call(body, in_specs, out_shape, limit, scratch=()):
    outs = out_shape if isinstance(out_shape, (list, tuple)) else [out_shape]
    specs = [in_vmem] * len(outs)
    return pl.pallas_call(
        body,
        in_specs=in_specs,
        out_specs=specs if isinstance(out_shape, (list, tuple)) else specs[0],
        out_shape=out_shape,
        scratch_shapes=list(scratch),
        compiler_params=pltpu.CompilerParams(vmem_limit_bytes=limit * mib),
    )


def together(*arrays):
    return lax.optimization_barrier(arrays)


def load(place, *arrays):
    count = len(arrays)

    def body(place_ref, *refs):
        token, sems = refs[-2:]
        copies = [
            pltpu.make_async_copy(refs[i], refs[count + i], sems.at[i]) for i in range(count)
        ]
        for copy in copies:
            copy.start()
        token[...] = jnp.zeros_like(token)
        for copy in copies:
            copy.wait()

    outs = kernel_call(
        body,
        [in_smem] + [in_hbm] * count,
        [pltpu.VMEM(a.shape, a.dtype) for a in arrays] + [shape_of((8, 128), jnp.float32)],
        2,
        [pltpu.SemaphoreType.DMA((count,))],
    )(place, *[in_place(x) for x in arrays])
    return [held(x) for x in outs[:count]] + [outs[count]]


def forward_first(order, pieces, rows, gate_weight, up_weight):
    parts, _, depth = pieces.shape
    units = gate_weight.shape[1]

    def body(order_ref, x_ref, gate_ref, up_ref, gate_out, up_out):
        for out, weight in ((gate_out, gate_ref), (up_out, up_ref)):
            total = jnp.zeros((rows, units), jnp.float32)
            for i in range(parts):
                at = pl.ds(pl.multiple_of(order_ref[i] * depth, depth), depth)
                total = total + dot32(x_ref[i, :rows], weight[at, :])
            out[...] = total

    return kernel_call(
        body,
        [in_smem, in_vmem, in_vmem, in_vmem],
        [shape_of((rows, units), jnp.float32)] * 2,
        6,
    )(order, pieces, gate_weight, up_weight)


def forward_rest(
    order, pieces, gate_part, up_part, gate_weight, up_weight, down_weight, to_relative, extra
):
    parts, _, depth = pieces.shape
    rows, units = gate_part.shape
    width = down_weight.shape[1]
    chunk = units // 4
    slots = 2

    def body(
        order_ref, x_ref, gate_in, up_in, gate_ref, up_ref, down_ref, one_hot, extra_ref,
        gate_out, up_out, own_out, other_out, held_ref, total_ref, sems,
    ):
        copies = [
            pltpu.make_async_copy(
                down_ref.at[pl.ds(i * chunk, chunk)], held_ref.at[i % slots], sems.at[i % slots]
            )
            for i in range(4)
        ]
        copies[0].start()
        copies[1].start()
        values = []
        for start, weight in ((gate_in, gate_ref), (up_in, up_ref)):
            total = start[...]
            for i in range(parts):
                at = pl.ds(pl.multiple_of(order_ref[parts + i] * depth, depth), depth)
                total = total + dot32(x_ref[i, :rows], weight[at, :])
            values.append(total)
        gate, up = values
        gate_out[:rows] = gate.astype(jnp.bfloat16)
        gate_out[rows:] = extra_ref[...]
        up_out[:rows] = up.astype(jnp.bfloat16)
        up_out[rows:] = extra_ref[...]
        hidden = (gate * sigmoid(gate) * up).astype(jnp.bfloat16)
        hidden = dot32(one_hot[...], hidden).astype(jnp.bfloat16)
        for i, copy in enumerate(copies):
            copy.wait()
            term = dot32(hidden[:, i * chunk : (i + 1) * chunk], held_ref[i % slots])
            total_ref[...] = term if i == 0 else total_ref[...] + term
            if i + slots < 4:
                copies[i + slots].start()
        own_out[...] = total_ref[: rows // 2].astype(jnp.bfloat16)
        other_out[...] = total_ref[rows // 2 :].astype(jnp.bfloat16)

    return kernel_call(
        body,
        [in_smem] + [in_vmem] * 5 + [in_hbm, in_vmem, in_vmem],
        [
            shape_of((rows + extra.shape[0], units)),
            shape_of((rows + extra.shape[0], units)),
            shape_of((rows // 2, width)),
            shape_of((rows // 2, width)),
        ],
        13,
        [
            pltpu.VMEM((slots, chunk, width), down_weight.dtype),
            pltpu.VMEM((rows, width), jnp.float32),
            pltpu.SemaphoreType.DMA((slots,)),
        ],
    )(
        order,
        pieces,
        gate_part,
        up_part,
        gate_weight,
        up_weight,
        in_place(down_weight),
        to_relative,
        extra,
    )


def input_blocks(place, order, first, second, rows, parts):
    half, _, depth = first.shape
    share = 2 * half // parts

    def body(place_ref, order_ref, first_ref, second_ref, *refs):
        outs, whole = refs[:parts], refs[parts]
        for j in range(2 * half):
            at = order_ref[j]
            to = pl.ds(pl.multiple_of((at % share) * depth, depth), depth)
            piece = first_ref[j, :rows] if j < half else second_ref[j - half, :rows]
            whole[at // share ^ place_ref[0], :, to] = piece
        for k, out in enumerate(outs):
            out[...] = whole[k]

    return kernel_call(
        body,
        [in_smem, in_smem, in_vmem, in_vmem],
        [shape_of((rows, share * depth))] * parts,
        4,
        [pltpu.VMEM((parts, rows, share * depth), first.dtype)],
    )(place, order, first, second)


def score_kernel(states, index_parts, inverse_norm, counts, dead, pad):
    pieces = len(states)
    rows, width = states[0].shape
    shard = index_parts[0].shape[0]
    chunk = width // 8

    def body(*refs):
        state_refs, refs = refs[:pieces], refs[pieces:]
        first, second, inverse_ref, counts_ref, dead_ref = refs[:5]
        outs = refs[5:]
        block = jnp.concatenate([r[...] for r in state_refs], axis=0)
        values = block.astype(jnp.float32)
        state_scale = inverse_temp / jnp.sqrt(jnp.sum(values * values, axis=1, keepdims=True) + eps)
        total = dead_ref[...]
        coeffs = []
        for k, index_ref in enumerate((first, second)):
            inverse = inverse_ref[:, k * shard : (k + 1) * shard]
            raw = dot32(block, index_ref[...], contract_last)
            weights = counts_ref[:, k * shard : (k + 1) * shard] * jnp.exp(raw * state_scale * inverse)
            total = total + jnp.sum(weights, axis=1, keepdims=True)
            coeffs.append((weights * inverse).astype(jnp.bfloat16))
        column = lax.broadcasted_iota(jnp.int32, (pieces * rows, pad), 1)
        last = jnp.where(column == 0, total, 0.0).astype(jnp.bfloat16)
        for p in range(pieces):
            outs[p][:, width:] = last[p * rows : (p + 1) * rows]
        for i in range(width // chunk):
            at = pl.ds(i * chunk, chunk)
            pull = dot32(coeffs[0], first[:, at]) + dot32(coeffs[1], second[:, at])
            for p in range(pieces):
                outs[p][:, at] = pull[p * rows : (p + 1) * rows].astype(jnp.bfloat16)

    return kernel_call(
        body,
        [in_vmem] * (pieces + 5),
        [shape_of((rows, width + pad))] * pieces,
        13,
    )(*states, *index_parts, inverse_norm, counts, dead)


def backward_hidden(order, own_rows, other_rows, down_weight, gate_act, up_act, to_relative, parts):
    half, width = own_rows.shape
    rows, units = 2 * half, down_weight.shape[0]
    part = width // parts
    chunk = 256 if units % 256 == 0 else units
    chunks = units // chunk
    slots = min(chunks, 3)

    def body(order_ref, own_ref, other_ref, down_ref, gate_ref, up_ref, one_hot, *refs):
        gate_out, up_out = refs[:2]
        outs, (grad_ref, held_ref, sems) = refs[2:-3], refs[-3:]
        spans = [pl.ds(i * chunk, chunk) for i in range(chunks)]
        copies = [
            pltpu.make_async_copy(down_ref.at[at], held_ref.at[i % slots], sems.at[i % slots])
            for i, at in enumerate(spans)
        ]
        for copy in copies[: max(slots - 1, 1)]:
            copy.start()
        grad = jnp.concatenate([own_ref[...], other_ref[...]], axis=0)
        grad_ref[...] = dot32(one_hot[...], grad, contract_first).astype(jnp.bfloat16)
        for k, out in enumerate(outs):
            out[:, units:] = grad_ref[:, pl.ds(pl.multiple_of(order_ref[k] * part, part), part)]
        for i, at in enumerate(spans):
            copies[i].wait()
            if i + slots - 1 < chunks and slots > 1:
                copies[i + slots - 1].start()
            hidden_grad = dot32(grad_ref[...], held_ref[i % slots], contract_last)
            for out in outs:
                out[:, at] = hidden_grad.astype(jnp.bfloat16)
            gate_out[:, at], up_out[:, at] = activation_grads(
                hidden_grad,
                gate_ref[:rows, at].astype(jnp.float32),
                up_ref[:rows, at].astype(jnp.float32),
            )

    outs = kernel_call(
        body,
        [in_smem, in_vmem, in_vmem, in_hbm, in_vmem, in_vmem, in_vmem],
        [shape_of((rows, units))] * 2 + [shape_of((rows, units + part))] * parts,
        13,
        [
            pltpu.VMEM((rows, width), jnp.bfloat16),
            pltpu.VMEM((slots, chunk, width), down_weight.dtype),
            pltpu.SemaphoreType.DMA((slots,)),
        ],
    )(order, own_rows, other_rows, in_place(down_weight), gate_act, up_act, to_relative)
    return outs[0], outs[1], outs[2:]


def backward_input(order, gate_grad, up_grad, gate_weight, up_weight):
    rows, units = gate_grad.shape
    width = gate_weight.shape[0]
    blocks = order.shape[0]
    depth = width // (2 * blocks)
    slots = 3

    def body(order_ref, gate_grad_ref, up_grad_ref, gate_ref, up_ref, out, held_ref, sems):
        def copies_of(n):
            at = pl.ds(pl.multiple_of(order_ref[n] * depth, depth), depth)
            return [
                pltpu.make_async_copy(source.at[at], held_ref.at[k, n % slots], sems.at[k, n % slots])
                for k, source in enumerate((gate_ref, up_ref))
            ]

        for n in range(slots - 1):
            for copy in copies_of(n):
                copy.start()
        for n in range(blocks):
            for copy in copies_of(n):
                copy.wait()
            if n + slots - 1 < blocks:
                for copy in copies_of(n + slots - 1):
                    copy.start()
            block = dot32(gate_grad_ref[...], held_ref[0, n % slots], contract_last) + dot32(
                up_grad_ref[...], held_ref[1, n % slots], contract_last
            )
            out[n] = block.astype(jnp.bfloat16)

    return kernel_call(
        body,
        [in_smem, in_vmem, in_vmem, in_hbm, in_hbm],
        shape_of((blocks, rows, depth)),
        14,
        [
            pltpu.VMEM((2, slots, depth, units), gate_weight.dtype),
            pltpu.SemaphoreType.DMA((2, slots)),
        ],
    )(order, gate_grad, up_grad, in_place(gate_weight), in_place(up_weight))


def weight_grads(input_columns, grads, gate_acts, up_acts):
    groups = len(grads)
    rows, units = grads[0].shape[0], gate_acts[0].shape[1]
    width = input_columns.shape[0]
    chunk = 256 if units % 256 == 0 else units

    def body(x_ref, *refs):
        at = pl.ds(0, units)
        if chunk < units:
            at = pl.ds(pl.multiple_of(pl.program_id(0) * chunk, chunk), chunk)
        hidden_grad, gate, up = (
            jnp.concatenate([r[:rows, at] for r in refs[k * groups : (k + 1) * groups]], axis=0)
            for k in range(3)
        )
        gate_out, up_out = refs[3 * groups :]
        gate_grad, up_grad = activation_grads(
            hidden_grad.astype(jnp.float32), gate.astype(jnp.float32), up.astype(jnp.float32)
        )
        gate_out[...] = dot32(x_ref[...], gate_grad).astype(jnp.bfloat16)
        up_out[...] = dot32(x_ref[...], up_grad).astype(jnp.bfloat16)

    return pl.pallas_call(
        body,
        grid=(units // chunk,),
        in_specs=[in_vmem] * (1 + 3 * groups),
        out_specs=[pl.BlockSpec((width, chunk), lambda i: (0, i))] * 2,
        out_shape=[shape_of((width, units))] * 2,
        compiler_params=pltpu.CompilerParams(vmem_limit_bytes=12 * mib),
    )(input_columns, *grads, *gate_acts, *up_acts)


def shards(
    mlp_input,
    residual_in,
    gate_weight,
    up_weight,
    down_weight,
    span_index,
    positive_keys,
    request_rows,
    request_counts,
    negative_slots,
):
    dp_count = lax.axis_size("dp")
    fsdp_count = lax.axis_size("fsdp")
    chips = fsdp_count // 2
    place = jnp.stack([lax.axis_index("dp"), lax.axis_index("fsdp")])
    my_dp, my_fsdp = place[:1], place[1:]
    me = my_dp * fsdp_count + my_fsdp
    width = span_index.shape[1]
    own_queries = negative_slots.shape[0]
    group_rows = mlp_input.shape[0]
    j = jnp.arange(fsdp_count, dtype=jnp.int32)
    fsdp_order = jnp.bitwise_xor(my_fsdp, 2 * (j % chips) + j // chips).astype(jnp.int32)
    dp_order = jnp.bitwise_xor(my_dp, jnp.arange(dp_count, dtype=jnp.int32)).astype(jnp.int32)
    to_relative = relative_order(my_fsdp, fsdp_count, own_queries)
    j = jnp.arange(dp_count * chips, dtype=jnp.int32)
    asker = jnp.bitwise_xor(my_dp, j // chips) * fsdp_count + jnp.bitwise_xor(
        my_fsdp, 2 * (j % chips)
    )
    both = jnp.concatenate([me, jnp.bitwise_xor(me, 1)])
    place, fsdp_order, dp_order, to_relative, asker, both = together(
        place, fsdp_order, dp_order, to_relative, asker, both
    )

    slot_cap, negatives = request_rows.shape[2], negative_slots.shape[1]
    slots = jnp.concatenate([negative_slots // slot_cap, negative_slots % slot_cap], axis=1)
    slots = jnp.pad(slots, ((0, 0), (0, mlp_input.shape[1] - 2 * negatives)))
    message = jnp.concatenate([mlp_input, slots.astype(jnp.bfloat16)], axis=0)
    gate_held, up_held, loaded = load(place, gate_weight, up_weight)
    first = gather_chips(message[None]) + loaded[0, 0].astype(jnp.bfloat16)
    second = swap_core(first)
    gate_part, up_part = forward_first(fsdp_order, first, group_rows, gate_held, up_held)
    gate_part, up_part, second, span_later = together(gate_part, up_part, second, span_index)
    units = up_weight.shape[1]
    bands = units // (2 * negatives)
    extra = [first[c, group_rows:, : 2 * negatives] for c in range(chips)]
    extra = [jnp.concatenate(extra[i : i + bands], axis=1) for i in range(0, chips, bands)]
    extra = [jnp.pad(x, ((0, 0), (0, units - x.shape[1]))) for x in extra]
    extra = jnp.concatenate(extra, axis=0)
    other_index = swap_core(span_later)
    gate_act, up_act, own_part, other_part = forward_rest(
        fsdp_order,
        second,
        gate_part,
        up_part,
        gate_held,
        up_held,
        down_weight,
        to_relative,
        extra,
    )

    near, far = 1, dp_count // 2
    own_part, other_part, other_index = together(own_part, other_part, other_index)
    own_part, received, request_rows, request_counts, span_later = together(
        own_part, swap_core(other_part), request_rows, request_counts, span_later
    )
    branch = add_up([own_part, received]).astype(jnp.bfloat16)

    tables = jnp.concatenate([request_rows[:, 0, :], request_counts], axis=1)[None]
    tables = gather_core(tables)
    top_state, gate_near, up_far, own_norm, other_index, tables = together(
        sum_chips(branch) + residual_in.astype(jnp.float32),
        swap(gate_act, "dp", near),
        swap(up_act, "dp", far),
        norm_of(span_later.astype(jnp.float32)),
        other_index,
        tables,
    )
    row_norm = norm_of(top_state)
    unit_rows = top_state / row_norm[:, None]

    states, gate_far, up_near, other_norm, span_later, tables, positive_keys = together(
        gather_chips(top_state.astype(jnp.bfloat16)),
        swap(
            jnp.concatenate([gate_act[:group_rows], gate_near[group_rows:]], axis=0), "dp", far
        ),
        swap(up_act, "dp", near),
        norm_of(other_index.astype(jnp.float32)),
        span_later,
        tables,
        positive_keys,
    )
    index_norm = jnp.concatenate([own_norm, other_norm], axis=0)
    slots = [x[group_rows:] for x in (gate_act, gate_near, up_far, gate_far)]
    slots = jnp.stack(slots).astype(jnp.int32)
    slots = [
        slots[
            :,
            c // bands * own_queries : (c // bands + 1) * own_queries,
            c % bands * 2 * negatives : (c % bands + 1) * 2 * negatives,
        ]
        for c in range(chips)
    ]
    slots = jnp.stack(slots, axis=1).reshape(dp_count * chips, own_queries, 2 * negatives)
    slots = slots[..., :negatives] * slot_cap + slots[..., negatives:]
    tables = jnp.take(tables, asker, axis=1)
    counts, dead = [], 0.0
    for k in range(2):
        shard_counts, shard_dead = use_counts(
            slots,
            tables[k, :, :-1],
            tables[k, :, -1],
            both[k : k + 1],
            span_index.shape[0],
        )
        counts.append(shard_counts)
        dead = dead + shard_dead
    counts = jnp.concatenate(counts, axis=1)
    states = [states] + [swap(states, "dp", k) for k in range(1, dp_count)]
    own_held, loaded = load(place, span_later)
    counts, dead, loaded, *states = together(counts, dead, loaded, *states)
    counts = counts + loaded[0, 0]
    index_parts = [own_held, held(other_index)]
    pulls = score_kernel(
        states, index_parts, (1.0 / index_norm)[None, :], counts, dead[:, None], 128
    )

    sums = add_up([pulls[0]] + [swap(pulls[k], "dp", k) for k in range(1, dp_count)])
    sums, gate_near, up_far = together(sums.astype(jnp.bfloat16), gate_near, up_far)
    sums, gate_last, up_last, first, second = together(
        sum_chips(sums), swap(gate_near, "dp", far), swap(up_far, "dp", near), first, second
    )
    negative_total = sums[:, width]
    positive_rows = positive_keys.astype(jnp.float32)
    positive_unit = positive_rows / norm_of(positive_rows)[:, None]
    positive_score = inverse_temp * jnp.sum(unit_rows * positive_unit, axis=-1)
    exp_total = jnp.exp(positive_score) + negative_total
    query_loss = jnp.log(exp_total) - positive_score
    pull = (sums[:, :width] - negative_total[:, None] * positive_unit) / exp_total[:, None]
    inner = jnp.sum(pull * unit_rows, axis=-1)
    head_grad = (
        inverse_temp * (pull - inner[:, None] * unit_rows) / row_norm[:, None]
    ).astype(jnp.bfloat16)

    blocks = input_blocks(place, fsdp_order, first, second, group_rows, dp_count)
    own_rows, *blocks = together(
        gather_chips(head_grad),
        blocks[0],
        swap(blocks[1], "dp", 1),
        swap(blocks[2], "dp", 2),
        blocks[3],
    )
    own_rows, other_rows = together(own_rows, swap_core(own_rows))
    gates = [gate_act, gate_near, gate_far, gate_last]
    ups = [up_act, up_near, up_far, up_last]
    hidden_all = jnp.concatenate(
        [
            (g * sigmoid(g) * u).astype(jnp.bfloat16).T
            for g, u in (
                (g[:group_rows].astype(jnp.float32), u[:group_rows].astype(jnp.float32))
                for g, u in zip(gates, ups)
            )
        ],
        axis=1,
    )

    own_gate_grad, own_up_grad, grads = backward_hidden(
        dp_order, own_rows, other_rows, down_weight, gate_act, up_act, to_relative, dp_count
    )
    own_gate_grad, own_up_grad, last_block = together(
        own_gate_grad, own_up_grad, swap(blocks[3], "dp", 3)
    )
    grads = [grads[0]] + [swap(grads[k], "dp", k) for k in range(1, dp_count)]
    other_blocks = backward_input(
        fsdp_order[chips:], own_gate_grad, own_up_grad, gate_weight, up_weight
    )
    other_blocks, own_gate_grad, own_up_grad = together(other_blocks, own_gate_grad, own_up_grad)
    own_blocks = backward_input(
        fsdp_order[:chips], own_gate_grad, own_up_grad, gate_weight, up_weight
    )
    own_blocks, received, *grads = together(own_blocks, swap_core(other_blocks), *grads)
    blocks_sum = add_up([own_blocks, received]).astype(jnp.bfloat16)
    input_grad = sum_chips(blocks_sum)[0].astype(jnp.bfloat16)

    grad_columns = jnp.concatenate([g[:, units:] for g in grads], axis=0)
    down_grad = dot32(hidden_all, grad_columns).astype(jnp.bfloat16)
    input_columns = jnp.concatenate(blocks[:3] + [last_block], axis=0).T
    gate_grad, up_grad = weight_grads(input_columns, grads, gates, ups)
    return (query_loss, input_grad, gate_grad, up_grad, down_grad)


def solution(mesh):
    return jax.shard_map(
        shards,
        mesh=mesh,
        in_specs=(
            P("dp", "fsdp"),
            P(("dp", "fsdp"), None),
            P(None, "fsdp"),
            P(None, "fsdp"),
            P("fsdp", None),
            P(("dp", "fsdp"), None),
            P(("dp", "fsdp"), None),
            P(None, ("dp", "fsdp"), None),
            P(None, ("dp", "fsdp")),
            P(("dp", "fsdp"), None),
        ),
        out_specs=(
            P(("dp", "fsdp")),
            P("dp", "fsdp"),
            P("dp", "fsdp"),
            P("dp", "fsdp"),
            P("fsdp", "dp"),
        ),
        check_vma=False,
    )
```

```python
import jax
import jax.numpy as jnp
from jax import lax
from jax.experimental import pallas as pl
from jax.experimental.pallas import tpu as pltpu
from jax.sharding import PartitionSpec as P

inverse_temp = 50.0
eps = 1e-06
contract_first = (((0,), (0,)), ((), ()))
contract_last = (((1,), (1,)), ((), ()))
every = ("dp", "fsdp")


def sigmoid(v):
    return 1.0 / (1.0 + jnp.exp(-v))


def activation_grads(hidden_grad, gate_act, up_act):
    gate = sigmoid(gate_act)
    gate_grad = hidden_grad * up_act * gate * (1.0 + gate_act * (1.0 - gate))
    return gate_grad.astype(jnp.bfloat16), (hidden_grad * gate_act * gate).astype(jnp.bfloat16)


def dot32(left, right, dims=(((1,), (0,)), ((), ()))):
    return lax.dot_general(left, right, dims, preferred_element_type=jnp.float32)


def norm_of(rows):
    return jnp.sqrt(jnp.sum(rows * rows, axis=-1) + eps)


def swap(x, axis, difference):
    pairs = [(i, i ^ difference) for i in range(lax.axis_size(axis))]
    return lax.ppermute(x, axis, pairs)


def swap_core(x):
    return swap(x, "fsdp", 1)


def gather_chips(x):
    chips = lax.axis_size("fsdp") // 2
    return jnp.concatenate([x] + [swap(x, "fsdp", 2 * j) for j in range(1, chips)], axis=0)


def gather_dp(x):
    return jnp.concatenate([x] + [swap(x, "dp", j) for j in range(1, lax.axis_size("dp"))], axis=0)


def gather_core(x):
    return jnp.concatenate([x, swap_core(x)], axis=0)


def add_up(pieces):
    total = pieces[0].astype(jnp.float32)
    for piece in pieces[1:]:
        total = total + piece.astype(jnp.float32)
    return total


def sum_core(x):
    rows = x.shape[0] // 2
    return add_up([x[:rows], swap_core(x[rows:])])


def sum_over(x, axis, parts, unit):
    rows = x.shape[0] // parts
    return add_up(
        [x[:rows]]
        + [swap(x[j * rows : (j + 1) * rows], axis, j * unit) for j in range(1, parts)]
    )


def sum_chips(x):
    return sum_over(x, "fsdp", lax.axis_size("fsdp") // 2, 2)


def sum_dp(x):
    return sum_over(x, "dp", lax.axis_size("dp"), 1)


def relative_order(mine, blocks, block_rows):
    rows = blocks * block_rows
    place = lax.broadcasted_iota(jnp.int32, (rows, rows), 0)
    block, row = place // block_rows, place % block_rows
    core, chip = block // (blocks // 2), block % (blocks // 2)
    source = jnp.bitwise_xor(mine[:, None], 2 * chip + core) * block_rows + row
    return (source == lax.broadcasted_iota(jnp.int32, (rows, rows), 1)).astype(jnp.bfloat16)


def use_counts(slots, row_table, count_table, shard, shard_rows):
    devices, queries, negatives = slots.shape
    slot_cap = row_table.shape[1]
    slot = lax.broadcasted_iota(jnp.int32, (1, 1, 1, slot_cap), 3) + shard[:, None, None, None] * slot_cap
    asked = jnp.sum((slots[..., None] == slot).astype(jnp.float32), axis=2)
    live = lax.broadcasted_iota(jnp.int32, (devices, 1, slot_cap), 2) < count_table[:, None, None]
    used = jnp.where(live, asked, 0.0)
    dead = jnp.sum(asked - used, axis=-1).reshape(devices * queries)
    row = lax.broadcasted_iota(jnp.int32, (1, 1, shard_rows), 2)
    picks = (row_table[:, :, None] == row).astype(jnp.bfloat16)
    counts = lax.dot_general(
        used.astype(jnp.bfloat16),
        picks,
        (((2,), (1,)), ((0,), (0,))),
        preferred_element_type=jnp.float32,
    )
    return counts.reshape(devices * queries, shard_rows), dead


in_vmem = pl.BlockSpec(memory_space=pltpu.VMEM)
in_smem = pl.BlockSpec(memory_space=pltpu.SMEM)
in_hbm = pl.BlockSpec(memory_space=pltpu.HBM)
mib = 2**20


def held(x):
    return pltpu.with_memory_space_constraint(x, pltpu.VMEM)


def in_place(x):
    return pltpu.with_memory_space_constraint(x, pltpu.HBM)


def shape_of(shape, dtype=jnp.bfloat16):
    return jax.ShapeDtypeStruct(shape, dtype)


def kernel_call(body, in_specs, out_shape, limit, scratch=()):
    outs = out_shape if isinstance(out_shape, (list, tuple)) else [out_shape]
    specs = [in_vmem] * len(outs)
    return pl.pallas_call(
        body,
        in_specs=in_specs,
        out_specs=specs if isinstance(out_shape, (list, tuple)) else specs[0],
        out_shape=out_shape,
        scratch_shapes=list(scratch),
        compiler_params=pltpu.CompilerParams(vmem_limit_bytes=limit * mib),
    )


def together(*arrays):
    return lax.optimization_barrier(arrays)


def load(place, *arrays):
    count = len(arrays)

    def body(place_ref, *refs):
        token, sems = refs[-2:]
        copies = [
            pltpu.make_async_copy(refs[i], refs[count + i], sems.at[i]) for i in range(count)
        ]
        for copy in copies:
            copy.start()
        token[...] = jnp.zeros_like(token)
        for copy in copies:
            copy.wait()

    outs = kernel_call(
        body,
        [in_smem] + [in_hbm] * count,
        [pltpu.VMEM(a.shape, a.dtype) for a in arrays] + [shape_of((8, 128), jnp.float32)],
        2,
        [pltpu.SemaphoreType.DMA((count,))],
    )(place, *[in_place(x) for x in arrays])
    return [held(x) for x in outs[:count]] + [outs[count]]


def forward_first(order, pieces, rows, gate_weight, up_weight):
    parts, _, depth = pieces.shape
    units = gate_weight.shape[1]

    def body(order_ref, x_ref, gate_ref, up_ref, gate_out, up_out):
        for out, weight in ((gate_out, gate_ref), (up_out, up_ref)):
            total = jnp.zeros((rows, units), jnp.float32)
            for i in range(parts):
                at = pl.ds(pl.multiple_of(order_ref[i] * depth, depth), depth)
                total = total + dot32(x_ref[i, :rows], weight[at, :])
            out[...] = total

    return kernel_call(
        body,
        [in_smem, in_vmem, in_vmem, in_vmem],
        [shape_of((rows, units), jnp.float32)] * 2,
        6,
    )(order, pieces, gate_weight, up_weight)


def forward_rest(
    order, pieces, gate_part, up_part, gate_weight, up_weight, down_weight, to_relative, extra
):
    parts, _, depth = pieces.shape
    rows, units = gate_part.shape
    width = down_weight.shape[1]
    chunk = width // 8
    slots = 4

    def body(
        order_ref, x_ref, gate_in, up_in, gate_ref, up_ref, down_ref, one_hot, extra_ref,
        gate_out, up_out, own_out, other_out, held_ref, sems,
    ):
        copies = [
            pltpu.make_async_copy(
                down_ref.at[:, pl.ds(i * chunk, chunk)], held_ref.at[i % slots], sems.at[i % slots]
            )
            for i in range(8)
        ]
        for copy in copies[:slots]:
            copy.start()
        values = []
        for start, weight in ((gate_in, gate_ref), (up_in, up_ref)):
            total = start[...]
            for i in range(parts):
                at = pl.ds(pl.multiple_of(order_ref[parts + i] * depth, depth), depth)
                total = total + dot32(x_ref[i, :rows], weight[at, :])
            values.append(total)
        gate, up = values
        gate_out[:rows] = gate.astype(jnp.bfloat16)
        gate_out[rows:] = extra_ref[...]
        up_out[:rows] = up.astype(jnp.bfloat16)
        up_out[rows:] = extra_ref[...]
        hidden = (gate * sigmoid(gate) * up).astype(jnp.bfloat16)
        hidden = dot32(one_hot[...], hidden).astype(jnp.bfloat16)
        for i, copy in enumerate(copies):
            copy.wait()
            at = pl.ds(i * chunk, chunk)
            total = dot32(hidden, held_ref[i % slots])
            if i + slots < 8:
                copies[i + slots].start()
            own_out[:, at] = total[: rows // 2].astype(jnp.bfloat16)
            other_out[:, at] = total[rows // 2 :].astype(jnp.bfloat16)

    return kernel_call(
        body,
        [in_smem] + [in_vmem] * 5 + [in_hbm, in_vmem, in_vmem],
        [
            shape_of((rows + extra.shape[0], units)),
            shape_of((rows + extra.shape[0], units)),
            shape_of((rows // 2, width)),
            shape_of((rows // 2, width)),
        ],
        13,
        [
            pltpu.VMEM((slots, units, chunk), down_weight.dtype),
            pltpu.SemaphoreType.DMA((slots,)),
        ],
    )(
        order,
        pieces,
        gate_part,
        up_part,
        gate_weight,
        up_weight,
        in_place(down_weight),
        to_relative,
        extra,
    )


def input_blocks(place, order, first, second, rows, parts):
    half, _, depth = first.shape
    share = 2 * half // parts

    def body(place_ref, order_ref, first_ref, second_ref, *refs):
        outs, whole = refs[:parts], refs[parts]
        for j in range(2 * half):
            at = order_ref[j]
            to = pl.ds(pl.multiple_of((at % share) * depth, depth), depth)
            piece = first_ref[j, :rows] if j < half else second_ref[j - half, :rows]
            whole[at // share ^ place_ref[0], :, to] = piece
        for k, out in enumerate(outs):
            out[...] = whole[k]

    return kernel_call(
        body,
        [in_smem, in_smem, in_vmem, in_vmem],
        [shape_of((rows, share * depth))] * parts,
        4,
        [pltpu.VMEM((parts, rows, share * depth), first.dtype)],
    )(place, order, first, second)


def score_kernel(states, index_parts, inverse_norm, counts, dead, pad):
    pieces = len(states)
    rows, width = states[0].shape
    shard = index_parts[0].shape[0]
    chunk = width // 8

    def body(*refs):
        state_refs, refs = refs[:pieces], refs[pieces:]
        sources, (inverse_ref, counts_ref, dead_ref) = refs[:2], refs[2:5]
        outs, (index_held, sems) = refs[5:-2], refs[-2:]
        copies = [
            pltpu.make_async_copy(source, index_held.at[k], sems.at[k])
            for k, source in enumerate(sources)
        ]
        for copy in copies:
            copy.start()
        block = jnp.concatenate([r[...] for r in state_refs], axis=0)
        values = block.astype(jnp.float32)
        state_scale = inverse_temp / jnp.sqrt(jnp.sum(values * values, axis=1, keepdims=True) + eps)
        total = dead_ref[...]
        coeffs = []
        for k, copy in enumerate(copies):
            copy.wait()
            inverse = inverse_ref[:, k * shard : (k + 1) * shard]
            raw = dot32(block, index_held[k], contract_last)
            weights = counts_ref[:, k * shard : (k + 1) * shard] * jnp.exp(raw * state_scale * inverse)
            total = total + jnp.sum(weights, axis=1, keepdims=True)
            coeffs.append((weights * inverse).astype(jnp.bfloat16))
        column = lax.broadcasted_iota(jnp.int32, (pieces * rows, pad), 1)
        last = jnp.where(column == 0, total, 0.0).astype(jnp.bfloat16)
        for p in range(pieces):
            outs[p][:, width:] = last[p * rows : (p + 1) * rows]
        for i in range(width // chunk):
            at = pl.ds(i * chunk, chunk)
            pull = dot32(coeffs[0], index_held[0, :, at]) + dot32(coeffs[1], index_held[1, :, at])
            for p in range(pieces):
                outs[p][:, at] = pull[p * rows : (p + 1) * rows].astype(jnp.bfloat16)

    return kernel_call(
        body,
        [in_vmem] * pieces + [in_hbm] * 2 + [in_vmem] * 3,
        [shape_of((rows, width + pad))] * pieces,
        20,
        [
            pltpu.VMEM((2, shard, width), index_parts[0].dtype),
            pltpu.SemaphoreType.DMA((2,)),
        ],
    )(*states, *[in_place(x) for x in index_parts], inverse_norm, counts, dead)


def backward_hidden(order, own_rows, other_rows, down_weight, gate_act, up_act, to_relative, parts):
    half, width = own_rows.shape
    rows, units = 2 * half, down_weight.shape[0]
    part = width // parts
    chunk = 256 if units % 256 == 0 else units
    chunks = units // chunk
    slots = min(chunks, 5)

    def body(order_ref, own_ref, other_ref, down_ref, gate_ref, up_ref, one_hot, *refs):
        gate_out, up_out = refs[:2]
        outs, (grad_ref, turned_ref, held_ref, sems) = refs[2:-4], refs[-4:]
        spans = [pl.ds(i * chunk, chunk) for i in range(chunks)]
        copies = [
            pltpu.make_async_copy(down_ref.at[at], held_ref.at[i % slots], sems.at[i % slots])
            for i, at in enumerate(spans)
        ]
        for copy in copies[: max(slots - 1, 1)]:
            copy.start()
        grad = jnp.concatenate([own_ref[...], other_ref[...]], axis=0)
        grad_ref[...] = dot32(one_hot[...], grad, contract_first).astype(jnp.bfloat16)
        turned_ref[...] = grad_ref[...].T
        for k, out in enumerate(outs):
            out[:, units:] = grad_ref[:, pl.ds(pl.multiple_of(order_ref[k] * part, part), part)]
        for i, at in enumerate(spans):
            copies[i].wait()
            if i + slots - 1 < chunks and slots > 1:
                copies[i + slots - 1].start()
            hidden_grad = dot32(held_ref[i % slots], turned_ref[...]).T
            for out in outs:
                out[:, at] = hidden_grad.astype(jnp.bfloat16)
            gate_out[:, at], up_out[:, at] = activation_grads(
                hidden_grad,
                gate_ref[:rows, at].astype(jnp.float32),
                up_ref[:rows, at].astype(jnp.float32),
            )

    outs = kernel_call(
        body,
        [in_smem, in_vmem, in_vmem, in_hbm, in_vmem, in_vmem, in_vmem],
        [shape_of((rows, units))] * 2 + [shape_of((rows, units + part))] * parts,
        16,
        [
            pltpu.VMEM((rows, width), jnp.bfloat16),
            pltpu.VMEM((width, rows), jnp.bfloat16),
            pltpu.VMEM((slots, chunk, width), down_weight.dtype),
            pltpu.SemaphoreType.DMA((slots,)),
        ],
    )(order, own_rows, other_rows, in_place(down_weight), gate_act, up_act, to_relative)
    return outs[0], outs[1], outs[2:]


def backward_input(order, gate_grad, up_grad, gate_weight, up_weight):
    rows, units = gate_grad.shape
    width = gate_weight.shape[0]
    blocks = order.shape[0]
    depth = width // blocks
    half = blocks // 2
    slots = 4

    def body(order_ref, gate_grad_ref, up_grad_ref, gate_ref, up_ref, own_out, other_out, held_ref, sems):
        def copies_of(n):
            at = pl.ds(pl.multiple_of(order_ref[n] * depth, depth), depth)
            return [
                pltpu.make_async_copy(source.at[at], held_ref.at[k, n % slots], sems.at[k, n % slots])
                for k, source in enumerate((gate_ref, up_ref))
            ]

        for n in range(slots - 1):
            for copy in copies_of(n):
                copy.start()
        for n in range(blocks):
            for copy in copies_of(n):
                copy.wait()
            if n + slots - 1 < blocks:
                for copy in copies_of(n + slots - 1):
                    copy.start()
            block = dot32(gate_grad_ref[...], held_ref[0, n % slots], contract_last) + dot32(
                up_grad_ref[...], held_ref[1, n % slots], contract_last
            )
            out = own_out if n < half else other_out
            out[n % half] = block.astype(jnp.bfloat16)

    return kernel_call(
        body,
        [in_smem, in_vmem, in_vmem, in_hbm, in_hbm],
        [shape_of((half, rows, depth))] * 2,
        18,
        [
            pltpu.VMEM((2, slots, depth, units), gate_weight.dtype),
            pltpu.SemaphoreType.DMA((2, slots)),
        ],
    )(order, gate_grad, up_grad, in_place(gate_weight), in_place(up_weight))


def weight_grads(input_columns, grads, gate_acts, up_acts):
    groups = len(grads)
    rows, units = grads[0].shape[0], gate_acts[0].shape[1]
    width = input_columns[0].shape[1]
    chunk = 256 if units % 256 == 0 else units

    def body(*refs):
        columns, refs, turned = refs[:groups], refs[groups:-1], refs[-1]

        @pl.when(pl.program_id(0) == 0)
        def _():
            turned[...] = jnp.concatenate([r[...] for r in columns], axis=0).T

        at = pl.ds(0, units)
        if chunk < units:
            at = pl.ds(pl.multiple_of(pl.program_id(0) * chunk, chunk), chunk)
        hidden_grad, gate, up = (
            jnp.concatenate([r[:rows, at] for r in refs[k * groups : (k + 1) * groups]], axis=0)
            for k in range(3)
        )
        gate_out, up_out = refs[3 * groups :]
        gate_grad, up_grad = activation_grads(
            hidden_grad.astype(jnp.float32), gate.astype(jnp.float32), up.astype(jnp.float32)
        )
        gate_out[...] = dot32(turned[...], gate_grad).astype(jnp.bfloat16)
        up_out[...] = dot32(turned[...], up_grad).astype(jnp.bfloat16)

    return pl.pallas_call(
        body,
        grid=(units // chunk,),
        in_specs=[in_vmem] * (4 * groups),
        out_specs=[pl.BlockSpec((width, chunk), lambda i: (0, i))] * 2,
        out_shape=[shape_of((width, units))] * 2,
        scratch_shapes=[pltpu.VMEM((width, groups * rows), jnp.bfloat16)],
        compiler_params=pltpu.CompilerParams(vmem_limit_bytes=14 * mib),
    )(*input_columns, *grads, *gate_acts, *up_acts)


def down_grads(grads, gate_acts, up_acts):
    groups = len(grads)
    rows, units = grads[0].shape[0], gate_acts[0].shape[1]
    width = grads[0].shape[1] - units
    chunk = 256 if units % 256 == 0 else units

    def body(*refs):
        at = pl.ds(0, units)
        if chunk < units:
            at = pl.ds(pl.multiple_of(pl.program_id(0) * chunk, chunk), chunk)
        gate, up = (
            jnp.concatenate([r[:rows, at] for r in refs[k * groups : (k + 1) * groups]], axis=0)
            for k in (1, 2)
        )
        gate, up = gate.astype(jnp.float32), up.astype(jnp.float32)
        hidden = (gate * sigmoid(gate) * up).astype(jnp.bfloat16)
        head_grad = jnp.concatenate([r[:, units:] for r in refs[:groups]], axis=0)
        refs[-1][...] = dot32(hidden, head_grad, contract_first).astype(jnp.bfloat16)

    return pl.pallas_call(
        body,
        grid=(units // chunk,),
        in_specs=[in_vmem] * (3 * groups),
        out_specs=pl.BlockSpec((chunk, width), lambda i: (i, 0)),
        out_shape=shape_of((units, width)),
        compiler_params=pltpu.CompilerParams(vmem_limit_bytes=14 * mib),
    )(*grads, *gate_acts, *up_acts)


def shards(
    mlp_input,
    residual_in,
    gate_weight,
    up_weight,
    down_weight,
    span_index,
    positive_keys,
    request_rows,
    request_counts,
    negative_slots,
):
    dp_count = lax.axis_size("dp")
    fsdp_count = lax.axis_size("fsdp")
    chips = fsdp_count // 2
    place = jnp.stack([lax.axis_index("dp"), lax.axis_index("fsdp")])
    my_dp, my_fsdp = place[:1], place[1:]
    me = my_dp * fsdp_count + my_fsdp
    width = span_index.shape[1]
    own_queries = negative_slots.shape[0]
    group_rows = mlp_input.shape[0]
    j = jnp.arange(fsdp_count, dtype=jnp.int32)
    fsdp_order = jnp.bitwise_xor(my_fsdp, 2 * (j % chips) + j // chips).astype(jnp.int32)
    dp_order = jnp.bitwise_xor(my_dp, jnp.arange(dp_count, dtype=jnp.int32)).astype(jnp.int32)
    to_relative = relative_order(my_fsdp, fsdp_count, own_queries)
    j = jnp.arange(dp_count * chips, dtype=jnp.int32)
    asker = jnp.bitwise_xor(my_dp, j // chips) * fsdp_count + jnp.bitwise_xor(
        my_fsdp, 2 * (j % chips)
    )
    both = jnp.concatenate([me, jnp.bitwise_xor(me, 1)])
    place, fsdp_order, dp_order, to_relative, asker, both = together(
        place, fsdp_order, dp_order, to_relative, asker, both
    )

    slot_cap, negatives = request_rows.shape[2], negative_slots.shape[1]
    slots = jnp.concatenate([negative_slots // slot_cap, negative_slots % slot_cap], axis=1)
    slots = jnp.pad(slots, ((0, 0), (0, mlp_input.shape[1] - 2 * negatives)))
    message = jnp.concatenate([mlp_input, slots.astype(jnp.bfloat16)], axis=0)
    gate_held, up_held, loaded = load(place, gate_weight, up_weight)
    first = gather_chips(message[None]) + loaded[0, 0].astype(jnp.bfloat16)
    second = swap_core(first)
    gate_part, up_part = forward_first(fsdp_order, first, group_rows, gate_held, up_held)
    gate_part, up_part, second, span_later = together(gate_part, up_part, second, span_index)
    units = up_weight.shape[1]
    bands = units // (2 * negatives)
    extra = [first[c, group_rows:, : 2 * negatives] for c in range(chips)]
    extra = [jnp.concatenate(extra[i : i + bands], axis=1) for i in range(0, chips, bands)]
    extra = [jnp.pad(x, ((0, 0), (0, units - x.shape[1]))) for x in extra]
    extra = jnp.concatenate(extra, axis=0)
    other_index = swap_core(span_later)
    gate_act, up_act, own_part, other_part = forward_rest(
        fsdp_order,
        second,
        gate_part,
        up_part,
        gate_held,
        up_held,
        down_weight,
        to_relative,
        extra,
    )

    near, far = 1, dp_count // 2
    own_part, other_part, other_index = together(own_part, other_part, other_index)
    own_part, received, request_rows, request_counts, span_later = together(
        own_part, swap_core(other_part), request_rows, request_counts, span_later
    )
    branch = add_up([own_part, received]).astype(jnp.bfloat16)

    tables = jnp.concatenate([request_rows[:, 0, :], request_counts], axis=1)[None]
    tables = gather_core(tables)
    top_state, gate_near, up_far, span_later, other_index, tables = together(
        sum_chips(branch) + residual_in.astype(jnp.float32),
        swap(gate_act, "dp", near),
        swap(up_act, "dp", far),
        span_later,
        other_index,
        tables,
    )
    row_norm = norm_of(top_state)
    unit_rows = top_state / row_norm[:, None]

    states, last_slots, own_norm, other_norm, span_later, other_index, tables, positive_keys, asker, both = together(
        gather_chips(top_state.astype(jnp.bfloat16)),
        swap(gate_near[group_rows:], "dp", far),
        norm_of(span_later.astype(jnp.float32)),
        norm_of(other_index.astype(jnp.float32)),
        span_later,
        other_index,
        tables,
        positive_keys,
        asker,
        both,
    )
    index_norm = jnp.concatenate([own_norm, other_norm], axis=0)
    slots = [x[group_rows:] for x in (gate_act, gate_near, up_far)] + [last_slots]
    slots = jnp.stack(slots).astype(jnp.int32)
    slots = [
        slots[
            :,
            c // bands * own_queries : (c // bands + 1) * own_queries,
            c % bands * 2 * negatives : (c % bands + 1) * 2 * negatives,
        ]
        for c in range(chips)
    ]
    slots = jnp.stack(slots, axis=1).reshape(dp_count * chips, own_queries, 2 * negatives)
    slots = slots[..., :negatives] * slot_cap + slots[..., negatives:]
    tables = jnp.take(tables, asker, axis=1)
    counts, dead = [], 0.0
    for k in range(2):
        shard_counts, shard_dead = use_counts(
            slots,
            tables[k, :, :-1],
            tables[k, :, -1],
            both[k : k + 1],
            span_index.shape[0],
        )
        counts.append(shard_counts)
        dead = dead + shard_dead
    counts = jnp.concatenate(counts, axis=1)
    states = [states] + [swap(states, "dp", k) for k in range(1, dp_count)]
    counts, dead, *states = together(counts, dead, *states)
    index_parts = [span_later, other_index]
    pulls = score_kernel(
        states, index_parts, (1.0 / index_norm)[None, :], counts, dead[:, None], 128
    )

    sums = add_up([pulls[0]] + [swap(pulls[k], "dp", k) for k in range(1, dp_count)])
    sums, gate_act, up_act, first, second = together(
        sums.astype(jnp.bfloat16), gate_act, up_act, first, second
    )
    sums, gate_far, up_near, *blocks = together(
        sum_chips(sums),
        swap(gate_act, "dp", far),
        swap(up_act, "dp", near),
        *input_blocks(place, fsdp_order, first, second, group_rows, dp_count),
    )
    negative_total = sums[:, width]
    positive_rows = positive_keys.astype(jnp.float32)
    positive_unit = positive_rows / norm_of(positive_rows)[:, None]
    positive_score = inverse_temp * jnp.sum(unit_rows * positive_unit, axis=-1)
    exp_total = jnp.exp(positive_score) + negative_total
    query_loss = jnp.log(exp_total) - positive_score
    pull = (sums[:, :width] - negative_total[:, None] * positive_unit) / exp_total[:, None]
    inner = jnp.sum(pull * unit_rows, axis=-1)
    head_grad = (
        inverse_temp * (pull - inner[:, None] * unit_rows) / row_norm[:, None]
    ).astype(jnp.bfloat16)

    head_grad, gate_near, up_far = together(head_grad, gate_near, up_far)
    own_rows, gate_last, up_last = together(
        gather_chips(head_grad), swap(gate_near, "dp", far), swap(up_far, "dp", near)
    )
    other_rows = swap_core(own_rows)
    gates = [gate_act, gate_near, gate_far, gate_last]
    ups = [up_act, up_near, up_far, up_last]
    own_gate_grad, own_up_grad, grads = backward_hidden(
        dp_order, own_rows, other_rows, down_weight, gate_act, up_act, to_relative, dp_count
    )
    own_gate_grad, own_up_grad, *rest = together(
        own_gate_grad,
        own_up_grad,
        *grads,
        blocks[0],
        *[swap(blocks[k], "dp", k) for k in range(1, dp_count)],
    )
    grads, blocks = rest[:dp_count], rest[dp_count:]
    grads = [grads[0]] + [swap(grads[k], "dp", k) for k in range(1, dp_count)]
    own_blocks, other_blocks = backward_input(
        fsdp_order, own_gate_grad, own_up_grad, gate_weight, up_weight
    )
    own_blocks, other_blocks, *grads = together(own_blocks, other_blocks, *grads)
    received = swap_core(other_blocks)
    down_grad = down_grads(grads, gates, ups)
    own_blocks, received, down_grad = together(own_blocks, received, down_grad)
    blocks_sum = add_up([own_blocks, received]).astype(jnp.bfloat16)
    input_grad = sum_chips(blocks_sum)[0].astype(jnp.bfloat16)
    gate_grad, up_grad = weight_grads(blocks, grads, gates, ups)
    return (query_loss, input_grad, gate_grad, up_grad, down_grad)


def solution(mesh):
    return jax.shard_map(
        shards,
        mesh=mesh,
        in_specs=(
            P("dp", "fsdp"),
            P(("dp", "fsdp"), None),
            P(None, "fsdp"),
            P(None, "fsdp"),
            P("fsdp", None),
            P(("dp", "fsdp"), None),
            P(("dp", "fsdp"), None),
            P(None, ("dp", "fsdp"), None),
            P(None, ("dp", "fsdp")),
            P(("dp", "fsdp"), None),
        ),
        out_specs=(
            P(("dp", "fsdp")),
            P("dp", "fsdp"),
            P("dp", "fsdp"),
            P("dp", "fsdp"),
            P("fsdp", "dp"),
        ),
        check_vma=False,
    )
```

```python
import jax
import jax.numpy as jnp
from jax import lax
from jax.experimental import pallas as pl
from jax.experimental.pallas import tpu as pltpu
from jax.sharding import PartitionSpec as P

inverse_temp = 50.0
eps = 1e-06
contract_first = (((0,), (0,)), ((), ()))
contract_last = (((1,), (1,)), ((), ()))
every = ("dp", "fsdp")


def sigmoid(v):
    return 1.0 / (1.0 + jnp.exp(-v))


def activation_grads(hidden_grad, gate_act, up_act):
    gate = sigmoid(gate_act)
    gate_grad = hidden_grad * up_act * gate * (1.0 + gate_act * (1.0 - gate))
    return gate_grad.astype(jnp.bfloat16), (hidden_grad * gate_act * gate).astype(jnp.bfloat16)


def dot32(left, right, dims=(((1,), (0,)), ((), ()))):
    return lax.dot_general(left, right, dims, preferred_element_type=jnp.float32)


def norm_of(rows):
    return jnp.sqrt(jnp.sum(rows * rows, axis=-1) + eps)


def swap(x, axis, difference):
    pairs = [(i, i ^ difference) for i in range(lax.axis_size(axis))]
    return lax.ppermute(x, axis, pairs)


def swap_core(x):
    return swap(x, "fsdp", 1)


def gather_chips(x):
    chips = lax.axis_size("fsdp") // 2
    return jnp.concatenate([x] + [swap(x, "fsdp", 2 * j) for j in range(1, chips)], axis=0)


def gather_dp(x):
    return jnp.concatenate([x] + [swap(x, "dp", j) for j in range(1, lax.axis_size("dp"))], axis=0)


def gather_core(x):
    return jnp.concatenate([x, swap_core(x)], axis=0)


def add_up(pieces):
    total = pieces[0].astype(jnp.float32)
    for piece in pieces[1:]:
        total = total + piece.astype(jnp.float32)
    return total


def sum_core(x):
    rows = x.shape[0] // 2
    return add_up([x[:rows], swap_core(x[rows:])])


def sum_over(x, axis, parts, unit):
    rows = x.shape[0] // parts
    return add_up(
        [x[:rows]]
        + [swap(x[j * rows : (j + 1) * rows], axis, j * unit) for j in range(1, parts)]
    )


def sum_chips(x):
    return sum_over(x, "fsdp", lax.axis_size("fsdp") // 2, 2)


def sum_dp(x):
    return sum_over(x, "dp", lax.axis_size("dp"), 1)


def relative_order(mine, blocks, block_rows):
    rows = blocks * block_rows
    place = lax.broadcasted_iota(jnp.int32, (rows, rows), 0)
    block, row = place // block_rows, place % block_rows
    core, chip = block // (blocks // 2), block % (blocks // 2)
    source = jnp.bitwise_xor(mine[:, None], 2 * chip + core) * block_rows + row
    return (source == lax.broadcasted_iota(jnp.int32, (rows, rows), 1)).astype(jnp.bfloat16)


def use_counts(slots, row_table, count_table, shard, shard_rows):
    devices, queries, negatives = slots.shape
    slot_cap = row_table.shape[1]
    slot = lax.broadcasted_iota(jnp.int32, (1, 1, 1, slot_cap), 3) + shard[:, None, None, None] * slot_cap
    asked = jnp.sum((slots[..., None] == slot).astype(jnp.float32), axis=2)
    live = lax.broadcasted_iota(jnp.int32, (devices, 1, slot_cap), 2) < count_table[:, None, None]
    used = jnp.where(live, asked, 0.0)
    dead = jnp.sum(asked - used, axis=-1).reshape(devices * queries)
    row = lax.broadcasted_iota(jnp.int32, (1, 1, shard_rows), 2)
    picks = (row_table[:, :, None] == row).astype(jnp.bfloat16)
    counts = lax.dot_general(
        used.astype(jnp.bfloat16),
        picks,
        (((2,), (1,)), ((0,), (0,))),
        preferred_element_type=jnp.float32,
    )
    return counts.reshape(devices * queries, shard_rows), dead


in_vmem = pl.BlockSpec(memory_space=pltpu.VMEM)
in_smem = pl.BlockSpec(memory_space=pltpu.SMEM)
in_hbm = pl.BlockSpec(memory_space=pltpu.HBM)
mib = 2**20


def held(x):
    return pltpu.with_memory_space_constraint(x, pltpu.VMEM)


def in_place(x):
    return pltpu.with_memory_space_constraint(x, pltpu.HBM)


def shape_of(shape, dtype=jnp.bfloat16):
    return jax.ShapeDtypeStruct(shape, dtype)


def kernel_call(body, in_specs, out_shape, limit, scratch=()):
    outs = out_shape if isinstance(out_shape, (list, tuple)) else [out_shape]
    specs = [in_vmem] * len(outs)
    return pl.pallas_call(
        body,
        in_specs=in_specs,
        out_specs=specs if isinstance(out_shape, (list, tuple)) else specs[0],
        out_shape=out_shape,
        scratch_shapes=list(scratch),
        compiler_params=pltpu.CompilerParams(vmem_limit_bytes=limit * mib),
    )


def together(*arrays):
    return lax.optimization_barrier(arrays)


def row_copies(order_ref, wanted, sources, held_ref, sems):
    depth = held_ref.shape[2]
    groups = []
    for n, j in enumerate(wanted):
        at = pl.ds(pl.multiple_of(order_ref[j] * depth, depth), depth)
        groups.append(
            [
                pltpu.make_async_copy(source.at[at], held_ref.at[k, n], sems.at[k, n])
                for k, source in enumerate(sources)
            ]
        )
    return groups


def in_turn(groups, ahead):
    for group in groups[:ahead]:
        for copy in group:
            copy.start()
    for n, group in enumerate(groups):
        for copy in group:
            copy.wait()
        for copy in groups[n + ahead] if n + ahead < len(groups) else []:
            copy.start()
        yield n


def forward_part(order, pieces, wanted, rows, gate_weight, up_weight, *totals):
    depth, units = pieces.shape[2], gate_weight.shape[1]
    begun = len(totals)

    def body(order_ref, x_ref, gate_ref, up_ref, *refs):
        starts, outs, (held_ref, sems) = refs[:begun], refs[begun:-2], refs[-2:]
        copies = row_copies(order_ref, wanted, (gate_ref, up_ref), held_ref, sems)
        for n in in_turn(copies, 3):
            for k, out in enumerate(outs):
                term = dot32(x_ref[wanted[n], :rows], held_ref[k, n])
                if n:
                    term = term + out[...]
                elif begun:
                    term = term + starts[k][...]
                out[...] = term

    return kernel_call(
        body,
        [in_smem, in_vmem, in_hbm, in_hbm] + [in_vmem] * begun,
        [shape_of((rows, units), jnp.float32)] * 2,
        18,
        [
            pltpu.VMEM((2, len(wanted), depth, units), gate_weight.dtype),
            pltpu.SemaphoreType.DMA((2, len(wanted))),
        ],
    )(order, pieces, in_place(gate_weight), in_place(up_weight), *totals)


def forward_rest(
    order, pieces, gate_part, up_part, gate_weight, up_weight, down_weight, to_relative, extra
):
    parts, _, depth = pieces.shape
    rows, units = gate_part.shape
    width = down_weight.shape[1]
    chunk = width // 8
    wanted = range(parts, 2 * parts)

    def body(
        order_ref, x_ref, gate_in, up_in, gate_ref, up_ref, down_ref, one_hot, extra_ref,
        gate_out, up_out, own_out, other_out, held_ref, down_held, totals, sems, down_sems,
    ):
        copies = row_copies(order_ref, wanted, (gate_ref, up_ref), held_ref, sems)
        for i in range(8):
            at = pl.ds(i * chunk, chunk)
            copies.append(
                [pltpu.make_async_copy(down_ref.at[:, at], down_held.at[i], down_sems.at[i])]
            )
        hidden = None
        for n in in_turn(copies, 4):
            if n < parts:
                for k, start in enumerate((gate_in, up_in)):
                    term = dot32(x_ref[n, :rows], held_ref[k, n])
                    totals[k] = term + (totals[k] if n else start[...])
                continue
            if hidden is None:
                gate, up = totals[0], totals[1]
                gate_out[:rows] = gate.astype(jnp.bfloat16)
                gate_out[rows:] = extra_ref[...]
                up_out[:rows] = up.astype(jnp.bfloat16)
                up_out[rows:] = extra_ref[...]
                hidden = (gate * sigmoid(gate) * up).astype(jnp.bfloat16)
                hidden = dot32(one_hot[...], hidden).astype(jnp.bfloat16)
            at = pl.ds((n - parts) * chunk, chunk)
            total = dot32(hidden, down_held[n - parts])
            own_out[:, at] = total[: rows // 2].astype(jnp.bfloat16)
            other_out[:, at] = total[rows // 2 :].astype(jnp.bfloat16)

    return kernel_call(
        body,
        [in_smem] + [in_vmem] * 3 + [in_hbm] * 3 + [in_vmem] * 2,
        [shape_of((rows + extra.shape[0], units))] * 2 + [shape_of((rows // 2, width))] * 2,
        36,
        [
            pltpu.VMEM((2, parts, depth, units), gate_weight.dtype),
            pltpu.VMEM((8, units, chunk), down_weight.dtype),
            pltpu.VMEM((2, rows, units), jnp.float32),
            pltpu.SemaphoreType.DMA((2, parts)),
            pltpu.SemaphoreType.DMA((8,)),
        ],
    )(
        order,
        pieces,
        gate_part,
        up_part,
        in_place(gate_weight),
        in_place(up_weight),
        in_place(down_weight),
        to_relative,
        extra,
    )


def input_blocks(place, order, first, second, rows, parts):
    half, _, depth = first.shape
    share = 2 * half // parts

    def body(place_ref, order_ref, first_ref, second_ref, *refs):
        outs, whole = refs[:parts], refs[parts]
        for j in range(2 * half):
            at = order_ref[j]
            to = pl.ds(pl.multiple_of((at % share) * depth, depth), depth)
            piece = first_ref[j, :rows] if j < half else second_ref[j - half, :rows]
            whole[at // share ^ place_ref[0], :, to] = piece
        for k, out in enumerate(outs):
            out[...] = whole[k]

    return kernel_call(
        body,
        [in_smem, in_smem, in_vmem, in_vmem],
        [shape_of((rows, share * depth))] * parts,
        4,
        [pltpu.VMEM((parts, rows, share * depth), first.dtype)],
    )(place, order, first, second)


def score_kernel(states, index_parts, inverse_norm, counts, dead, pad):
    pieces = len(states)
    rows, width = states[0].shape
    shard = index_parts[0].shape[0]
    chunk = width // 8

    def body(*refs):
        state_refs, refs = refs[:pieces], refs[pieces:]
        sources, (inverse_ref, counts_ref, dead_ref) = refs[:2], refs[2:5]
        outs, (index_held, sems) = refs[5:-2], refs[-2:]
        copies = [
            pltpu.make_async_copy(source, index_held.at[k], sems.at[k])
            for k, source in enumerate(sources)
        ]
        for copy in copies:
            copy.start()
        block = jnp.concatenate([r[...] for r in state_refs], axis=0)
        values = block.astype(jnp.float32)
        state_scale = inverse_temp / jnp.sqrt(jnp.sum(values * values, axis=1, keepdims=True) + eps)
        total = dead_ref[...]
        coeffs = []
        for k, copy in enumerate(copies):
            copy.wait()
            inverse = inverse_ref[:, k * shard : (k + 1) * shard]
            raw = dot32(block, index_held[k], contract_last)
            weights = counts_ref[:, k * shard : (k + 1) * shard] * jnp.exp(raw * state_scale * inverse)
            total = total + jnp.sum(weights, axis=1, keepdims=True)
            coeffs.append((weights * inverse).astype(jnp.bfloat16))
        column = lax.broadcasted_iota(jnp.int32, (pieces * rows, pad), 1)
        last = jnp.where(column == 0, total, 0.0).astype(jnp.bfloat16)
        for p in range(pieces):
            outs[p][:, width:] = last[p * rows : (p + 1) * rows]
        for i in range(width // chunk):
            at = pl.ds(i * chunk, chunk)
            pull = dot32(coeffs[0], index_held[0, :, at]) + dot32(coeffs[1], index_held[1, :, at])
            for p in range(pieces):
                outs[p][:, at] = pull[p * rows : (p + 1) * rows].astype(jnp.bfloat16)

    return kernel_call(
        body,
        [in_vmem] * pieces + [in_hbm] * 2 + [in_vmem] * 3,
        [shape_of((rows, width + pad))] * pieces,
        20,
        [
            pltpu.VMEM((2, shard, width), index_parts[0].dtype),
            pltpu.SemaphoreType.DMA((2,)),
        ],
    )(*states, *[in_place(x) for x in index_parts], inverse_norm, counts, dead)


def backward_hidden(order, own_rows, other_rows, down_weight, gate_act, up_act, to_relative, parts):
    half, width = own_rows.shape
    rows, units = 2 * half, down_weight.shape[0]
    part = width // parts
    chunk = 256 if units % 256 == 0 else units
    chunks = units // chunk
    slots = min(chunks, 5)

    def body(order_ref, own_ref, other_ref, down_ref, gate_ref, up_ref, one_hot, *refs):
        gate_out, up_out = refs[:2]
        outs, (grad_ref, turned_ref, held_ref, sems) = refs[2:-4], refs[-4:]
        spans = [pl.ds(i * chunk, chunk) for i in range(chunks)]
        copies = [
            pltpu.make_async_copy(down_ref.at[at], held_ref.at[i % slots], sems.at[i % slots])
            for i, at in enumerate(spans)
        ]
        for copy in copies[: max(slots - 1, 1)]:
            copy.start()
        grad = jnp.concatenate([own_ref[...], other_ref[...]], axis=0)
        grad_ref[...] = dot32(one_hot[...], grad, contract_first).astype(jnp.bfloat16)
        turned_ref[...] = grad_ref[...].T
        for k, out in enumerate(outs):
            out[:, units:] = grad_ref[:, pl.ds(pl.multiple_of(order_ref[k] * part, part), part)]
        for i, at in enumerate(spans):
            copies[i].wait()
            if i + slots - 1 < chunks and slots > 1:
                copies[i + slots - 1].start()
            hidden_grad = dot32(held_ref[i % slots], turned_ref[...]).T
            for out in outs:
                out[:, at] = hidden_grad.astype(jnp.bfloat16)
            gate_out[:, at], up_out[:, at] = activation_grads(
                hidden_grad,
                gate_ref[:rows, at].astype(jnp.float32),
                up_ref[:rows, at].astype(jnp.float32),
            )

    outs = kernel_call(
        body,
        [in_smem, in_vmem, in_vmem, in_hbm, in_vmem, in_vmem, in_vmem],
        [shape_of((rows, units))] * 2 + [shape_of((rows, units + part))] * parts,
        16,
        [
            pltpu.VMEM((rows, width), jnp.bfloat16),
            pltpu.VMEM((width, rows), jnp.bfloat16),
            pltpu.VMEM((slots, chunk, width), down_weight.dtype),
            pltpu.SemaphoreType.DMA((slots,)),
        ],
    )(order, own_rows, other_rows, in_place(down_weight), gate_act, up_act, to_relative)
    return outs[0], outs[1], outs[2:]


def backward_input(order, gate_grad, up_grad, gate_weight, up_weight):
    rows, units = gate_grad.shape
    width = gate_weight.shape[0]
    blocks = order.shape[0]
    depth = width // blocks
    half = blocks // 2
    slots = 4

    def body(order_ref, gate_grad_ref, up_grad_ref, gate_ref, up_ref, own_out, other_out, held_ref, sems):
        def copies_of(n):
            at = pl.ds(pl.multiple_of(order_ref[n] * depth, depth), depth)
            return [
                pltpu.make_async_copy(source.at[at], held_ref.at[k, n % slots], sems.at[k, n % slots])
                for k, source in enumerate((gate_ref, up_ref))
            ]

        for n in range(slots - 1):
            for copy in copies_of(n):
                copy.start()
        for n in range(blocks):
            for copy in copies_of(n):
                copy.wait()
            if n + slots - 1 < blocks:
                for copy in copies_of(n + slots - 1):
                    copy.start()
            block = dot32(gate_grad_ref[...], held_ref[0, n % slots], contract_last) + dot32(
                up_grad_ref[...], held_ref[1, n % slots], contract_last
            )
            out = own_out if n < half else other_out
            out[n % half] = block.astype(jnp.bfloat16)

    return kernel_call(
        body,
        [in_smem, in_vmem, in_vmem, in_hbm, in_hbm],
        [shape_of((half, rows, depth))] * 2,
        18,
        [
            pltpu.VMEM((2, slots, depth, units), gate_weight.dtype),
            pltpu.SemaphoreType.DMA((2, slots)),
        ],
    )(order, gate_grad, up_grad, in_place(gate_weight), in_place(up_weight))


def weight_grads(input_columns, grads, gate_acts, up_acts):
    groups = len(grads)
    rows, units = grads[0].shape[0], gate_acts[0].shape[1]
    width = input_columns[0].shape[1]
    chunk = 256 if units % 256 == 0 else units

    def body(*refs):
        columns, refs, turned = refs[:groups], refs[groups:-1], refs[-1]

        @pl.when(pl.program_id(0) == 0)
        def _():
            turned[...] = jnp.concatenate([r[...] for r in columns], axis=0).T

        at = pl.ds(0, units)
        if chunk < units:
            at = pl.ds(pl.multiple_of(pl.program_id(0) * chunk, chunk), chunk)
        hidden_grad, gate, up = (
            jnp.concatenate([r[:rows, at] for r in refs[k * groups : (k + 1) * groups]], axis=0)
            for k in range(3)
        )
        gate_out, up_out = refs[3 * groups :]
        gate_grad, up_grad = activation_grads(
            hidden_grad.astype(jnp.float32), gate.astype(jnp.float32), up.astype(jnp.float32)
        )
        gate_out[...] = dot32(turned[...], gate_grad).astype(jnp.bfloat16)
        up_out[...] = dot32(turned[...], up_grad).astype(jnp.bfloat16)

    return pl.pallas_call(
        body,
        grid=(units // chunk,),
        in_specs=[in_vmem] * (4 * groups),
        out_specs=[pl.BlockSpec((width, chunk), lambda i: (0, i))] * 2,
        out_shape=[shape_of((width, units))] * 2,
        scratch_shapes=[pltpu.VMEM((width, groups * rows), jnp.bfloat16)],
        compiler_params=pltpu.CompilerParams(vmem_limit_bytes=14 * mib),
    )(*input_columns, *grads, *gate_acts, *up_acts)


def down_grads(grads, gate_acts, up_acts):
    groups = len(grads)
    rows, units = grads[0].shape[0], gate_acts[0].shape[1]
    width = grads[0].shape[1] - units
    chunk = 256 if units % 256 == 0 else units

    def body(*refs):
        at = pl.ds(0, units)
        if chunk < units:
            at = pl.ds(pl.multiple_of(pl.program_id(0) * chunk, chunk), chunk)
        gate, up = (
            jnp.concatenate([r[:rows, at] for r in refs[k * groups : (k + 1) * groups]], axis=0)
            for k in (1, 2)
        )
        gate, up = gate.astype(jnp.float32), up.astype(jnp.float32)
        hidden = (gate * sigmoid(gate) * up).astype(jnp.bfloat16)
        head_grad = jnp.concatenate([r[:, units:] for r in refs[:groups]], axis=0)
        refs[-1][...] = dot32(hidden, head_grad, contract_first).astype(jnp.bfloat16)

    return pl.pallas_call(
        body,
        grid=(units // chunk,),
        in_specs=[in_vmem] * (3 * groups),
        out_specs=pl.BlockSpec((chunk, width), lambda i: (i, 0)),
        out_shape=shape_of((units, width)),
        compiler_params=pltpu.CompilerParams(vmem_limit_bytes=14 * mib),
    )(*grads, *gate_acts, *up_acts)


def shards(
    mlp_input,
    residual_in,
    gate_weight,
    up_weight,
    down_weight,
    span_index,
    positive_keys,
    request_rows,
    request_counts,
    negative_slots,
):
    dp_count = lax.axis_size("dp")
    fsdp_count = lax.axis_size("fsdp")
    chips = fsdp_count // 2
    place = jnp.stack([lax.axis_index("dp"), lax.axis_index("fsdp")])
    my_dp, my_fsdp = place[:1], place[1:]
    me = my_dp * fsdp_count + my_fsdp
    width = span_index.shape[1]
    own_queries = negative_slots.shape[0]
    group_rows = mlp_input.shape[0]
    j = jnp.arange(fsdp_count, dtype=jnp.int32)
    fsdp_order = jnp.bitwise_xor(my_fsdp, 2 * (j % chips) + j // chips).astype(jnp.int32)
    dp_order = jnp.bitwise_xor(my_dp, jnp.arange(dp_count, dtype=jnp.int32)).astype(jnp.int32)
    to_relative = relative_order(my_fsdp, fsdp_count, own_queries)
    j = jnp.arange(dp_count * chips, dtype=jnp.int32)
    asker = jnp.bitwise_xor(my_dp, j // chips) * fsdp_count + jnp.bitwise_xor(
        my_fsdp, 2 * (j % chips)
    )
    both = jnp.concatenate([me, jnp.bitwise_xor(me, 1)])
    place, fsdp_order, dp_order, to_relative, asker, both = together(
        place, fsdp_order, dp_order, to_relative, asker, both
    )

    slot_cap, negatives = request_rows.shape[2], negative_slots.shape[1]
    slots = jnp.concatenate([negative_slots // slot_cap, negative_slots % slot_cap], axis=1)
    slots = jnp.pad(slots, ((0, 0), (0, mlp_input.shape[1] - 2 * negatives)))
    message = jnp.concatenate([mlp_input, slots.astype(jnp.bfloat16)], axis=0)
    parts = forward_part(fsdp_order, message[None], (0,), group_rows, gate_weight, up_weight)
    first, *parts = together(gather_chips(message[None]), *parts)
    second = swap_core(first)
    gate_part, up_part = forward_part(
        fsdp_order, first, tuple(range(1, chips)), group_rows, gate_weight, up_weight, *parts
    )
    gate_part, up_part, second, span_later = together(gate_part, up_part, second, span_index)
    units = up_weight.shape[1]
    bands = units // (2 * negatives)
    extra = [first[c, group_rows:, : 2 * negatives] for c in range(chips)]
    extra = [jnp.concatenate(extra[i : i + bands], axis=1) for i in range(0, chips, bands)]
    extra = [jnp.pad(x, ((0, 0), (0, units - x.shape[1]))) for x in extra]
    extra = jnp.concatenate(extra, axis=0)
    other_index = swap_core(span_later)
    gate_act, up_act, own_part, other_part = forward_rest(
        fsdp_order,
        second,
        gate_part,
        up_part,
        gate_weight,
        up_weight,
        down_weight,
        to_relative,
        extra,
    )

    near, far = 1, dp_count // 2
    own_part, other_part, other_index = together(own_part, other_part, other_index)
    own_part, received, gate_act, up_act, request_rows, request_counts, span_later = together(
        own_part, swap_core(other_part), gate_act, up_act, request_rows, request_counts, span_later
    )
    branch = add_up([own_part, received]).astype(jnp.bfloat16)

    tables = jnp.concatenate([request_rows[:, 0, :], request_counts], axis=1)[None]
    tables = gather_core(tables)
    top_state, gate_near, up_far, span_later, other_index, tables = together(
        sum_chips(branch) + residual_in.astype(jnp.float32),
        swap(gate_act, "dp", near),
        swap(up_act, "dp", far),
        span_later,
        other_index,
        tables,
    )
    row_norm = norm_of(top_state)
    unit_rows = top_state / row_norm[:, None]

    states, last_slots, own_norm, other_norm, span_later, other_index, tables, positive_keys, asker, both = together(
        gather_chips(top_state.astype(jnp.bfloat16)),
        swap(gate_near[group_rows:], "dp", far),
        norm_of(span_later.astype(jnp.float32)),
        norm_of(other_index.astype(jnp.float32)),
        span_later,
        other_index,
        tables,
        positive_keys,
        asker,
        both,
    )
    index_norm = jnp.concatenate([own_norm, other_norm], axis=0)
    slots = [x[group_rows:] for x in (gate_act, gate_near, up_far)] + [last_slots]
    slots = jnp.stack(slots).astype(jnp.int32)
    slots = [
        slots[
            :,
            c // bands * own_queries : (c // bands + 1) * own_queries,
            c % bands * 2 * negatives : (c % bands + 1) * 2 * negatives,
        ]
        for c in range(chips)
    ]
    slots = jnp.stack(slots, axis=1).reshape(dp_count * chips, own_queries, 2 * negatives)
    slots = slots[..., :negatives] * slot_cap + slots[..., negatives:]
    tables = jnp.take(tables, asker, axis=1)
    counts, dead = [], 0.0
    for k in range(2):
        shard_counts, shard_dead = use_counts(
            slots,
            tables[k, :, :-1],
            tables[k, :, -1],
            both[k : k + 1],
            span_index.shape[0],
        )
        counts.append(shard_counts)
        dead = dead + shard_dead
    counts = jnp.concatenate(counts, axis=1)
    states = [states] + [swap(states, "dp", k) for k in range(1, dp_count)]
    counts, dead, *states = together(counts, dead, *states)
    index_parts = [span_later, other_index]
    pulls = score_kernel(
        states, index_parts, (1.0 / index_norm)[None, :], counts, dead[:, None], 128
    )

    sums = add_up([pulls[0]] + [swap(pulls[k], "dp", k) for k in range(1, dp_count)])
    sums, gate_act, up_act, first, second = together(
        sums.astype(jnp.bfloat16), gate_act, up_act, first, second
    )
    sums, gate_far, up_near, *blocks = together(
        sum_chips(sums),
        swap(gate_act, "dp", far),
        swap(up_act, "dp", near),
        *input_blocks(place, fsdp_order, first, second, group_rows, dp_count),
    )
    negative_total = sums[:, width]
    positive_rows = positive_keys.astype(jnp.float32)
    positive_unit = positive_rows / norm_of(positive_rows)[:, None]
    positive_score = inverse_temp * jnp.sum(unit_rows * positive_unit, axis=-1)
    exp_total = jnp.exp(positive_score) + negative_total
    query_loss = jnp.log(exp_total) - positive_score
    pull = (sums[:, :width] - negative_total[:, None] * positive_unit) / exp_total[:, None]
    inner = jnp.sum(pull * unit_rows, axis=-1)
    head_grad = (
        inverse_temp * (pull - inner[:, None] * unit_rows) / row_norm[:, None]
    ).astype(jnp.bfloat16)

    own_rows, block_near, block_far, gate_near, up_far = together(
        gather_chips(head_grad),
        swap(blocks[near], "dp", near),
        swap(blocks[far], "dp", far),
        gate_near,
        up_far,
    )
    gate_last, up_last = swap(gate_near, "dp", far), swap(up_far, "dp", near)
    other_rows = swap_core(own_rows)
    own_gate_grad, own_up_grad, grads = backward_hidden(
        dp_order, own_rows, other_rows, down_weight, gate_act, up_act, to_relative, dp_count
    )
    own_gate_grad, own_up_grad, gate_last, up_last, block_last, *grads = together(
        own_gate_grad,
        own_up_grad,
        gate_last,
        up_last,
        swap(blocks[near + far], "dp", near + far),
        *grads,
    )
    blocks = [blocks[0], block_near, block_far, block_last]
    gates = [gate_act, gate_near, gate_far, gate_last]
    ups = [up_act, up_near, up_far, up_last]
    grads = [grads[0]] + [swap(grads[k], "dp", k) for k in range(1, dp_count)]
    own_blocks, other_blocks = backward_input(
        fsdp_order, own_gate_grad, own_up_grad, gate_weight, up_weight
    )
    own_blocks, other_blocks, *grads = together(own_blocks, other_blocks, *grads)
    received = swap_core(other_blocks)
    down_grad = down_grads(grads, gates, ups)
    own_blocks, received, down_grad = together(own_blocks, received, down_grad)
    blocks_sum = add_up([own_blocks, received]).astype(jnp.bfloat16)
    input_grad = sum_chips(blocks_sum)[0].astype(jnp.bfloat16)
    gate_grad, up_grad = weight_grads(blocks, grads, gates, ups)
    return (query_loss, input_grad, gate_grad, up_grad, down_grad)


def solution(mesh):
    return jax.shard_map(
        shards,
        mesh=mesh,
        in_specs=(
            P("dp", "fsdp"),
            P(("dp", "fsdp"), None),
            P(None, "fsdp"),
            P(None, "fsdp"),
            P("fsdp", None),
            P(("dp", "fsdp"), None),
            P(("dp", "fsdp"), None),
            P(None, ("dp", "fsdp"), None),
            P(None, ("dp", "fsdp")),
            P(("dp", "fsdp"), None),
        ),
        out_specs=(
            P(("dp", "fsdp")),
            P("dp", "fsdp"),
            P("dp", "fsdp"),
            P("dp", "fsdp"),
            P("fsdp", "dp"),
        ),
        check_vma=False,
    )
```

```python
import jax
import jax.numpy as jnp
from jax import lax
from jax.experimental import pallas as pl
from jax.experimental.pallas import tpu as pltpu
from jax.sharding import PartitionSpec as P

inverse_temp = 50.0
eps = 1e-06
contract_first = (((0,), (0,)), ((), ()))
contract_last = (((1,), (1,)), ((), ()))
every = ("dp", "fsdp")


def sigmoid(v):
    return 1.0 / (1.0 + jnp.exp(-v))


def activation_grads(hidden_grad, gate_act, up_act):
    gate = sigmoid(gate_act)
    gate_grad = hidden_grad * up_act * gate * (1.0 + gate_act * (1.0 - gate))
    return gate_grad.astype(jnp.bfloat16), (hidden_grad * gate_act * gate).astype(jnp.bfloat16)


def dot32(left, right, dims=(((1,), (0,)), ((), ()))):
    return lax.dot_general(left, right, dims, preferred_element_type=jnp.float32)


def norm_of(rows):
    return jnp.sqrt(jnp.sum(rows * rows, axis=-1) + eps)


def swap(x, axis, difference):
    pairs = [(i, i ^ difference) for i in range(lax.axis_size(axis))]
    return lax.ppermute(x, axis, pairs)


def swap_core(x):
    return swap(x, "fsdp", 1)


def gather_chips(x):
    chips = lax.axis_size("fsdp") // 2
    return jnp.concatenate([x] + [swap(x, "fsdp", 2 * j) for j in range(1, chips)], axis=0)


def gather_dp(x):
    return jnp.concatenate([x] + [swap(x, "dp", j) for j in range(1, lax.axis_size("dp"))], axis=0)


def gather_core(x):
    return jnp.concatenate([x, swap_core(x)], axis=0)


def add_up(pieces):
    total = pieces[0].astype(jnp.float32)
    for piece in pieces[1:]:
        total = total + piece.astype(jnp.float32)
    return total


def sum_core(x):
    rows = x.shape[0] // 2
    return add_up([x[:rows], swap_core(x[rows:])])


def sum_over(x, axis, parts, unit):
    rows = x.shape[0] // parts
    return add_up(
        [x[:rows]]
        + [swap(x[j * rows : (j + 1) * rows], axis, j * unit) for j in range(1, parts)]
    )


def sum_chips(x):
    return sum_over(x, "fsdp", lax.axis_size("fsdp") // 2, 2)


def sum_dp(x):
    return sum_over(x, "dp", lax.axis_size("dp"), 1)


def relative_order(mine, blocks, block_rows):
    rows = blocks * block_rows
    place = lax.broadcasted_iota(jnp.int32, (rows, rows), 0)
    block, row = place // block_rows, place % block_rows
    core, chip = block // (blocks // 2), block % (blocks // 2)
    source = jnp.bitwise_xor(mine[:, None], 2 * chip + core) * block_rows + row
    return (source == lax.broadcasted_iota(jnp.int32, (rows, rows), 1)).astype(jnp.bfloat16)


def use_counts(slots, row_table, count_table, shard, shard_rows):
    devices, queries, negatives = slots.shape
    slot_cap = row_table.shape[1]
    slot = lax.broadcasted_iota(jnp.int32, (1, 1, 1, slot_cap), 3) + shard[:, None, None, None] * slot_cap
    asked = jnp.sum((slots[..., None] == slot).astype(jnp.float32), axis=2)
    live = lax.broadcasted_iota(jnp.int32, (devices, 1, slot_cap), 2) < count_table[:, None, None]
    used = jnp.where(live, asked, 0.0)
    dead = jnp.sum(asked - used, axis=-1).reshape(devices * queries)
    row = lax.broadcasted_iota(jnp.int32, (1, 1, shard_rows), 2)
    picks = (row_table[:, :, None] == row).astype(jnp.bfloat16)
    counts = lax.dot_general(
        used.astype(jnp.bfloat16),
        picks,
        (((2,), (1,)), ((0,), (0,))),
        preferred_element_type=jnp.float32,
    )
    return counts.reshape(devices * queries, shard_rows), dead


in_vmem = pl.BlockSpec(memory_space=pltpu.VMEM)
in_smem = pl.BlockSpec(memory_space=pltpu.SMEM)
in_hbm = pl.BlockSpec(memory_space=pltpu.HBM)
mib = 2**20


def held(x):
    return pltpu.with_memory_space_constraint(x, pltpu.VMEM)


def in_place(x):
    return pltpu.with_memory_space_constraint(x, pltpu.HBM)


def shape_of(shape, dtype=jnp.bfloat16):
    return jax.ShapeDtypeStruct(shape, dtype)


def kernel_call(body, in_specs, out_shape, limit, scratch=()):
    outs = out_shape if isinstance(out_shape, (list, tuple)) else [out_shape]
    specs = [in_vmem] * len(outs)
    return pl.pallas_call(
        body,
        in_specs=in_specs,
        out_specs=specs if isinstance(out_shape, (list, tuple)) else specs[0],
        out_shape=out_shape,
        scratch_shapes=list(scratch),
        compiler_params=pltpu.CompilerParams(vmem_limit_bytes=limit * mib),
    )


def together(*arrays):
    return lax.optimization_barrier(arrays)


def row_copies(order_ref, wanted, sources, held_ref, sems):
    depth = held_ref.shape[2]
    groups = []
    for n, j in enumerate(wanted):
        at = pl.ds(pl.multiple_of(order_ref[j] * depth, depth), depth)
        groups.append(
            [
                pltpu.make_async_copy(source.at[at], held_ref.at[k, n], sems.at[k, n])
                for k, source in enumerate(sources)
            ]
        )
    return groups


def in_turn(groups, ahead):
    for group in groups[:ahead]:
        for copy in group:
            copy.start()
    for n, group in enumerate(groups):
        for copy in group:
            copy.wait()
        for copy in groups[n + ahead] if n + ahead < len(groups) else []:
            copy.start()
        yield n


def forward_part(order, pieces, wanted, rows, gate_weight, up_weight, *totals):
    depth, units = pieces.shape[2], gate_weight.shape[1]
    begun = len(totals)

    def body(order_ref, x_ref, gate_ref, up_ref, *refs):
        starts, outs, (held_ref, sems) = refs[:begun], refs[begun:-2], refs[-2:]
        copies = row_copies(order_ref, wanted, (gate_ref, up_ref), held_ref, sems)
        for n in in_turn(copies, 3):
            for k, out in enumerate(outs):
                term = dot32(x_ref[wanted[n], :rows], held_ref[k, n])
                if n:
                    term = term + out[...]
                elif begun:
                    term = term + starts[k][...]
                out[...] = term

    return kernel_call(
        body,
        [in_smem, in_vmem, in_hbm, in_hbm] + [in_vmem] * begun,
        [shape_of((rows, units), jnp.float32)] * 2,
        18,
        [
            pltpu.VMEM((2, len(wanted), depth, units), gate_weight.dtype),
            pltpu.SemaphoreType.DMA((2, len(wanted))),
        ],
    )(order, pieces, in_place(gate_weight), in_place(up_weight), *totals)


def forward_rest(
    order, pieces, gate_part, up_part, gate_weight, up_weight, down_weight, to_relative, extra
):
    parts, _, depth = pieces.shape
    rows, units = gate_part.shape
    width = down_weight.shape[1]
    chunk = width // 8
    wanted = range(parts, 2 * parts)

    def body(
        order_ref, x_ref, gate_in, up_in, gate_ref, up_ref, down_ref, one_hot, extra_ref,
        gate_out, up_out, own_out, other_out, held_ref, down_held, totals, sems, down_sems,
    ):
        copies = row_copies(order_ref, wanted, (gate_ref, up_ref), held_ref, sems)
        for i in range(8):
            at = pl.ds(i * chunk, chunk)
            copies.append(
                [pltpu.make_async_copy(down_ref.at[:, at], down_held.at[i], down_sems.at[i])]
            )
        hidden = None
        for n in in_turn(copies, 4):
            if n < parts:
                for k, start in enumerate((gate_in, up_in)):
                    term = dot32(x_ref[n, :rows], held_ref[k, n])
                    totals[k] = term + (totals[k] if n else start[...])
                continue
            if hidden is None:
                gate, up = totals[0], totals[1]
                gate_out[:rows] = gate.astype(jnp.bfloat16)
                gate_out[rows:] = extra_ref[...]
                up_out[:rows] = up.astype(jnp.bfloat16)
                up_out[rows:] = extra_ref[...]
                hidden = (gate * sigmoid(gate) * up).astype(jnp.bfloat16)
                hidden = dot32(one_hot[...], hidden).astype(jnp.bfloat16)
            at = pl.ds((n - parts) * chunk, chunk)
            total = dot32(hidden, down_held[n - parts])
            own_out[:, at] = total[: rows // 2].astype(jnp.bfloat16)
            other_out[:, at] = total[rows // 2 :].astype(jnp.bfloat16)

    return kernel_call(
        body,
        [in_smem] + [in_vmem] * 3 + [in_hbm] * 3 + [in_vmem] * 2,
        [shape_of((rows + extra.shape[0], units))] * 2 + [shape_of((rows // 2, width))] * 2,
        36,
        [
            pltpu.VMEM((2, parts, depth, units), gate_weight.dtype),
            pltpu.VMEM((8, units, chunk), down_weight.dtype),
            pltpu.VMEM((2, rows, units), jnp.float32),
            pltpu.SemaphoreType.DMA((2, parts)),
            pltpu.SemaphoreType.DMA((8,)),
        ],
    )(
        order,
        pieces,
        gate_part,
        up_part,
        in_place(gate_weight),
        in_place(up_weight),
        in_place(down_weight),
        to_relative,
        extra,
    )


def input_blocks(place, order, first, second, rows, parts):
    half, _, depth = first.shape
    share = 2 * half // parts

    def body(place_ref, order_ref, first_ref, second_ref, *refs):
        outs, whole = refs[:parts], refs[parts]
        for j in range(2 * half):
            at = order_ref[j]
            to = pl.ds(pl.multiple_of((at % share) * depth, depth), depth)
            piece = first_ref[j, :rows] if j < half else second_ref[j - half, :rows]
            whole[at // share ^ place_ref[0], :, to] = piece
        for k, out in enumerate(outs):
            out[...] = whole[k]

    return kernel_call(
        body,
        [in_smem, in_smem, in_vmem, in_vmem],
        [shape_of((rows, share * depth))] * parts,
        4,
        [pltpu.VMEM((parts, rows, share * depth), first.dtype)],
    )(place, order, first, second)


def score_kernel(states, index_parts, inverse_norm, counts, dead, pad):
    pieces = len(states)
    rows, width = states[0].shape
    shard = index_parts[0].shape[0]
    chunk = width // 8

    def body(*refs):
        state_refs, refs = refs[:pieces], refs[pieces:]
        sources, (inverse_ref, counts_ref, dead_ref) = refs[:2], refs[2:5]
        outs, (index_held, sems) = refs[5:-2], refs[-2:]
        copies = [
            pltpu.make_async_copy(source, index_held.at[k], sems.at[k])
            for k, source in enumerate(sources)
        ]
        for copy in copies:
            copy.start()
        block = jnp.concatenate([r[...] for r in state_refs], axis=0)
        values = block.astype(jnp.float32)
        state_scale = inverse_temp / jnp.sqrt(jnp.sum(values * values, axis=1, keepdims=True) + eps)
        total = dead_ref[...]
        coeffs = []
        for k, copy in enumerate(copies):
            copy.wait()
            inverse = inverse_ref[:, k * shard : (k + 1) * shard]
            raw = dot32(block, index_held[k], contract_last)
            weights = counts_ref[:, k * shard : (k + 1) * shard] * jnp.exp(raw * state_scale * inverse)
            total = total + jnp.sum(weights, axis=1, keepdims=True)
            coeffs.append((weights * inverse).astype(jnp.bfloat16))
        column = lax.broadcasted_iota(jnp.int32, (pieces * rows, pad), 1)
        last = jnp.where(column == 0, total, 0.0).astype(jnp.bfloat16)
        for p in range(pieces):
            outs[p][:, width:] = last[p * rows : (p + 1) * rows]
        for i in range(width // chunk):
            at = pl.ds(i * chunk, chunk)
            pull = dot32(coeffs[0], index_held[0, :, at]) + dot32(coeffs[1], index_held[1, :, at])
            for p in range(pieces):
                outs[p][:, at] = pull[p * rows : (p + 1) * rows].astype(jnp.bfloat16)

    return kernel_call(
        body,
        [in_vmem] * pieces + [in_hbm] * 2 + [in_vmem] * 3,
        [shape_of((rows, width + pad))] * pieces,
        20,
        [
            pltpu.VMEM((2, shard, width), index_parts[0].dtype),
            pltpu.SemaphoreType.DMA((2,)),
        ],
    )(*states, *[in_place(x) for x in index_parts], inverse_norm, counts, dead)


def backward_hidden(order, own_rows, other_rows, down_weight, gate_act, up_act, to_relative, parts):
    half, width = own_rows.shape
    rows, units = 2 * half, down_weight.shape[0]
    part = width // parts
    chunk = 256 if units % 256 == 0 else units
    chunks = units // chunk
    slots = min(chunks, 5)

    def body(order_ref, own_ref, other_ref, down_ref, gate_ref, up_ref, one_hot, *refs):
        gate_out, up_out = refs[:2]
        outs, (grad_ref, turned_ref, held_ref, sems) = refs[2:-4], refs[-4:]
        spans = [pl.ds(i * chunk, chunk) for i in range(chunks)]
        copies = [
            pltpu.make_async_copy(down_ref.at[at], held_ref.at[i % slots], sems.at[i % slots])
            for i, at in enumerate(spans)
        ]
        for copy in copies[: max(slots - 1, 1)]:
            copy.start()
        grad = jnp.concatenate([own_ref[...], other_ref[...]], axis=0)
        grad_ref[...] = dot32(one_hot[...], grad, contract_first).astype(jnp.bfloat16)
        turned_ref[...] = grad_ref[...].T
        for k, out in enumerate(outs):
            out[:, units:] = grad_ref[:, pl.ds(pl.multiple_of(order_ref[k] * part, part), part)]
        for i, at in enumerate(spans):
            copies[i].wait()
            if i + slots - 1 < chunks and slots > 1:
                copies[i + slots - 1].start()
            hidden_grad = dot32(held_ref[i % slots], turned_ref[...]).T
            for out in outs:
                out[:, at] = hidden_grad.astype(jnp.bfloat16)
            gate_out[:, at], up_out[:, at] = activation_grads(
                hidden_grad,
                gate_ref[:rows, at].astype(jnp.float32),
                up_ref[:rows, at].astype(jnp.float32),
            )

    outs = kernel_call(
        body,
        [in_smem, in_vmem, in_vmem, in_hbm, in_vmem, in_vmem, in_vmem],
        [shape_of((rows, units))] * 2 + [shape_of((rows, units + part))] * parts,
        16,
        [
            pltpu.VMEM((rows, width), jnp.bfloat16),
            pltpu.VMEM((width, rows), jnp.bfloat16),
            pltpu.VMEM((slots, chunk, width), down_weight.dtype),
            pltpu.SemaphoreType.DMA((slots,)),
        ],
    )(order, own_rows, other_rows, in_place(down_weight), gate_act, up_act, to_relative)
    return outs[0], outs[1], outs[2:]


def backward_input(order, gate_grad, up_grad, gate_weight, up_weight):
    rows, units = gate_grad.shape
    width = gate_weight.shape[0]
    blocks = order.shape[0]
    depth = width // blocks
    half = blocks // 2
    slots = 4

    def body(order_ref, gate_grad_ref, up_grad_ref, gate_ref, up_ref, own_out, other_out, held_ref, sems):
        def copies_of(n):
            at = pl.ds(pl.multiple_of(order_ref[n] * depth, depth), depth)
            return [
                pltpu.make_async_copy(source.at[at], held_ref.at[k, n % slots], sems.at[k, n % slots])
                for k, source in enumerate((gate_ref, up_ref))
            ]

        for n in range(slots - 1):
            for copy in copies_of(n):
                copy.start()
        for n in range(blocks):
            for copy in copies_of(n):
                copy.wait()
            if n + slots - 1 < blocks:
                for copy in copies_of(n + slots - 1):
                    copy.start()
            block = dot32(gate_grad_ref[...], held_ref[0, n % slots], contract_last) + dot32(
                up_grad_ref[...], held_ref[1, n % slots], contract_last
            )
            out = own_out if n < half else other_out
            out[n % half] = block.astype(jnp.bfloat16)

    return kernel_call(
        body,
        [in_smem, in_vmem, in_vmem, in_hbm, in_hbm],
        [shape_of((half, rows, depth))] * 2,
        18,
        [
            pltpu.VMEM((2, slots, depth, units), gate_weight.dtype),
            pltpu.SemaphoreType.DMA((2, slots)),
        ],
    )(order, gate_grad, up_grad, in_place(gate_weight), in_place(up_weight))


def weight_grads(input_columns, grads, gate_acts, up_acts):
    groups = len(grads)
    rows, units = grads[0].shape[0], gate_acts[0].shape[1]
    width = input_columns[0].shape[1]
    chunk = 256 if units % 256 == 0 else units
    chunks = units // chunk

    def body(*refs):
        columns, refs = refs[:groups], refs[groups:]
        (gate_out, up_out, turned, made, sems), refs = refs[3 * groups :], refs[: 3 * groups]
        turned[...] = jnp.concatenate([r[...] for r in columns], axis=0).T
        copies = []
        for i in range(chunks):
            at = pl.ds(i * chunk, chunk)
            hidden_grad, gate, up = (
                jnp.concatenate([r[:rows, at] for r in refs[k * groups : (k + 1) * groups]], axis=0)
                for k in range(3)
            )
            both = activation_grads(
                hidden_grad.astype(jnp.float32), gate.astype(jnp.float32), up.astype(jnp.float32)
            )
            for k, out in enumerate((gate_out, up_out)):
                made[k, i] = dot32(turned[...], both[k]).astype(jnp.bfloat16)
                copies.append(
                    pltpu.make_async_copy(made.at[k, i], out.at[:, at], sems.at[k, i])
                )
                copies[-1].start()
        for copy in copies:
            copy.wait()

    return pl.pallas_call(
        body,
        in_specs=[in_vmem] * (4 * groups),
        out_specs=[pl.BlockSpec(memory_space=pl.ANY)] * 2,
        out_shape=[shape_of((width, units))] * 2,
        scratch_shapes=[
            pltpu.VMEM((width, groups * rows), jnp.bfloat16),
            pltpu.VMEM((2, chunks, width, chunk), jnp.bfloat16),
            pltpu.SemaphoreType.DMA((2, chunks)),
        ],
        compiler_params=pltpu.CompilerParams(vmem_limit_bytes=18 * mib),
    )(*input_columns, *grads, *gate_acts, *up_acts)


def down_grads(grads, gate_acts, up_acts):
    groups = len(grads)
    rows, units = grads[0].shape[0], gate_acts[0].shape[1]
    width = grads[0].shape[1] - units
    chunk = 256 if units % 256 == 0 else units
    chunks = units // chunk

    def body(*refs):
        (out, made, sems), refs = refs[3 * groups :], refs[: 3 * groups]
        head_grad = jnp.concatenate([r[:, units:] for r in refs[:groups]], axis=0)
        copies = []
        for i in range(chunks):
            at = pl.ds(i * chunk, chunk)
            gate, up = (
                jnp.concatenate([r[:rows, at] for r in refs[k * groups : (k + 1) * groups]], axis=0)
                for k in (1, 2)
            )
            gate, up = gate.astype(jnp.float32), up.astype(jnp.float32)
            hidden = (gate * sigmoid(gate) * up).astype(jnp.bfloat16)
            made[i] = dot32(hidden, head_grad, contract_first).astype(jnp.bfloat16)
            copies.append(pltpu.make_async_copy(made.at[i], out.at[at], sems.at[i]))
            copies[-1].start()
        for copy in copies:
            copy.wait()

    return pl.pallas_call(
        body,
        in_specs=[in_vmem] * (3 * groups),
        out_specs=pl.BlockSpec(memory_space=pl.ANY),
        out_shape=shape_of((units, width)),
        scratch_shapes=[
            pltpu.VMEM((chunks, chunk, width), jnp.bfloat16),
            pltpu.SemaphoreType.DMA((chunks,)),
        ],
        compiler_params=pltpu.CompilerParams(vmem_limit_bytes=14 * mib),
    )(*grads, *gate_acts, *up_acts)


def shards(
    mlp_input,
    residual_in,
    gate_weight,
    up_weight,
    down_weight,
    span_index,
    positive_keys,
    request_rows,
    request_counts,
    negative_slots,
):
    dp_count = lax.axis_size("dp")
    fsdp_count = lax.axis_size("fsdp")
    chips = fsdp_count // 2
    place = jnp.stack([lax.axis_index("dp"), lax.axis_index("fsdp")])
    my_dp, my_fsdp = place[:1], place[1:]
    me = my_dp * fsdp_count + my_fsdp
    width = span_index.shape[1]
    own_queries = negative_slots.shape[0]
    group_rows = mlp_input.shape[0]
    j = jnp.arange(fsdp_count, dtype=jnp.int32)
    fsdp_order = jnp.bitwise_xor(my_fsdp, 2 * (j % chips) + j // chips).astype(jnp.int32)
    dp_order = jnp.bitwise_xor(my_dp, jnp.arange(dp_count, dtype=jnp.int32)).astype(jnp.int32)
    to_relative = relative_order(my_fsdp, fsdp_count, own_queries)
    j = jnp.arange(dp_count * chips, dtype=jnp.int32)
    asker = jnp.bitwise_xor(my_dp, j // chips) * fsdp_count + jnp.bitwise_xor(
        my_fsdp, 2 * (j % chips)
    )
    both = jnp.concatenate([me, jnp.bitwise_xor(me, 1)])
    place, fsdp_order, dp_order, to_relative, asker, both = together(
        place, fsdp_order, dp_order, to_relative, asker, both
    )

    slot_cap, negatives = request_rows.shape[2], negative_slots.shape[1]
    slots = jnp.concatenate([negative_slots // slot_cap, negative_slots % slot_cap], axis=1)
    slots = jnp.pad(slots, ((0, 0), (0, mlp_input.shape[1] - 2 * negatives)))
    message = jnp.concatenate([mlp_input, slots.astype(jnp.bfloat16)], axis=0)
    parts = forward_part(fsdp_order, message[None], (0,), group_rows, gate_weight, up_weight)
    first, *parts = together(gather_chips(message[None]), *parts)
    second = swap_core(first)
    gate_part, up_part = forward_part(
        fsdp_order, first, tuple(range(1, chips)), group_rows, gate_weight, up_weight, *parts
    )
    tables = jnp.concatenate([request_rows[:, 0, :], request_counts], axis=1)[None]
    gate_part, up_part, second, span_later, tables = together(
        gate_part, up_part, second, span_index, gather_core(tables)
    )
    units = up_weight.shape[1]
    bands = units // (2 * negatives)
    extra = [first[c, group_rows:, : 2 * negatives] for c in range(chips)]
    extra = [jnp.concatenate(extra[i : i + bands], axis=1) for i in range(0, chips, bands)]
    extra = [jnp.pad(x, ((0, 0), (0, units - x.shape[1]))) for x in extra]
    extra = jnp.concatenate(extra, axis=0)
    other_index = swap_core(span_later)
    gate_act, up_act, own_part, other_part = forward_rest(
        fsdp_order,
        second,
        gate_part,
        up_part,
        gate_weight,
        up_weight,
        down_weight,
        to_relative,
        extra,
    )

    near, far = 1, dp_count // 2
    own_part, other_part, other_index = together(own_part, other_part, other_index)
    own_part, received, gate_act, up_act, span_later, tables = together(
        own_part, swap_core(other_part), gate_act, up_act, span_later, tables
    )
    branch = add_up([own_part, received]).astype(jnp.bfloat16)

    tables = jnp.take(tables, asker, axis=1)
    top_state, gate_near, up_far, own_norm, span_later, other_index, tables = together(
        sum_chips(branch) + residual_in.astype(jnp.float32),
        swap(gate_act, "dp", near),
        swap(up_act, "dp", far),
        norm_of(span_later.astype(jnp.float32)),
        span_later,
        other_index,
        tables,
    )
    row_norm = norm_of(top_state)
    unit_rows = top_state / row_norm[:, None]

    states, last_slots, other_norm, span_later, other_index, tables, positive_keys, both = together(
        gather_chips(top_state.astype(jnp.bfloat16)),
        swap(gate_near[group_rows:], "dp", far),
        swap_core(own_norm),
        span_later,
        other_index,
        tables,
        positive_keys,
        both,
    )
    index_norm = jnp.concatenate([own_norm, other_norm], axis=0)
    slots = [x[group_rows:] for x in (gate_act, gate_near, up_far)] + [last_slots]
    slots = jnp.stack(slots).astype(jnp.int32)
    slots = [
        slots[
            :,
            c // bands * own_queries : (c // bands + 1) * own_queries,
            c % bands * 2 * negatives : (c % bands + 1) * 2 * negatives,
        ]
        for c in range(chips)
    ]
    slots = jnp.stack(slots, axis=1).reshape(dp_count * chips, own_queries, 2 * negatives)
    slots = slots[..., :negatives] * slot_cap + slots[..., negatives:]
    counts, dead = [], 0.0
    for k in range(2):
        shard_counts, shard_dead = use_counts(
            slots,
            tables[k, :, :-1],
            tables[k, :, -1],
            both[k : k + 1],
            span_index.shape[0],
        )
        counts.append(shard_counts)
        dead = dead + shard_dead
    counts = jnp.concatenate(counts, axis=1)
    states = [states] + [swap(states, "dp", k) for k in range(1, dp_count)]
    counts, dead, *states = together(counts, dead, *states)
    index_parts = [span_later, other_index]
    pulls = score_kernel(
        states, index_parts, (1.0 / index_norm)[None, :], counts, dead[:, None], 128
    )

    sums = add_up([pulls[0]] + [swap(pulls[k], "dp", k) for k in range(1, dp_count)])
    sums, gate_act, up_act, first, second = together(
        sums.astype(jnp.bfloat16), gate_act, up_act, first, second
    )
    sums, gate_far, up_near, *blocks = together(
        sum_chips(sums),
        swap(gate_act, "dp", far),
        swap(up_act, "dp", near),
        *input_blocks(place, fsdp_order, first, second, group_rows, dp_count),
    )
    negative_total = sums[:, width]
    positive_rows = positive_keys.astype(jnp.float32)
    positive_unit = positive_rows / norm_of(positive_rows)[:, None]
    positive_score = inverse_temp * jnp.sum(unit_rows * positive_unit, axis=-1)
    exp_total = jnp.exp(positive_score) + negative_total
    query_loss = jnp.log(exp_total) - positive_score
    pull = (sums[:, :width] - negative_total[:, None] * positive_unit) / exp_total[:, None]
    inner = jnp.sum(pull * unit_rows, axis=-1)
    head_grad = (
        inverse_temp * (pull - inner[:, None] * unit_rows) / row_norm[:, None]
    ).astype(jnp.bfloat16)

    own_rows, block_near, block_far, gate_near, up_far = together(
        gather_chips(head_grad),
        swap(blocks[near], "dp", near),
        swap(blocks[far], "dp", far),
        gate_near,
        up_far,
    )
    gate_last, up_last = swap(gate_near, "dp", far), swap(up_far, "dp", near)
    other_rows = swap_core(own_rows)
    own_gate_grad, own_up_grad, grads = backward_hidden(
        dp_order, own_rows, other_rows, down_weight, gate_act, up_act, to_relative, dp_count
    )
    own_gate_grad, own_up_grad, gate_last, up_last, block_last, *grads = together(
        own_gate_grad,
        own_up_grad,
        gate_last,
        up_last,
        swap(blocks[near + far], "dp", near + far),
        *grads,
    )
    blocks = [blocks[0], block_near, block_far, block_last]
    gates = [gate_act, gate_near, gate_far, gate_last]
    ups = [up_act, up_near, up_far, up_last]
    grads = [grads[0]] + [swap(grads[k], "dp", k) for k in range(1, dp_count)]
    own_blocks, other_blocks = backward_input(
        fsdp_order, own_gate_grad, own_up_grad, gate_weight, up_weight
    )
    own_blocks, other_blocks, *grads = together(own_blocks, other_blocks, *grads)
    received = swap_core(other_blocks)
    down_grad = down_grads(grads, gates, ups)
    own_blocks, received, down_grad = together(own_blocks, received, down_grad)
    blocks_sum = add_up([own_blocks, received]).astype(jnp.bfloat16)
    input_grad = sum_chips(blocks_sum)[0].astype(jnp.bfloat16)
    gate_grad, up_grad = weight_grads(blocks, grads, gates, ups)
    return (query_loss, input_grad, gate_grad, up_grad, down_grad)


def solution(mesh):
    return jax.shard_map(
        shards,
        mesh=mesh,
        in_specs=(
            P("dp", "fsdp"),
            P(("dp", "fsdp"), None),
            P(None, "fsdp"),
            P(None, "fsdp"),
            P("fsdp", None),
            P(("dp", "fsdp"), None),
            P(("dp", "fsdp"), None),
            P(None, ("dp", "fsdp"), None),
            P(None, ("dp", "fsdp")),
            P(("dp", "fsdp"), None),
        ),
        out_specs=(
            P(("dp", "fsdp")),
            P("dp", "fsdp"),
            P("dp", "fsdp"),
            P("dp", "fsdp"),
            P("fsdp", "dp"),
        ),
        check_vma=False,
    )
```

```python
import jax
import jax.numpy as jnp
from jax import lax
from jax.experimental import pallas as pl
from jax.experimental.pallas import tpu as pltpu
from jax.sharding import PartitionSpec as P

inverse_temp = 50.0
eps = 1e-06
contract_first = (((0,), (0,)), ((), ()))
contract_last = (((1,), (1,)), ((), ()))
every = ("dp", "fsdp")


def sigmoid(v):
    return 1.0 / (1.0 + jnp.exp(-v))


def activation_grads(hidden_grad, gate_act, up_act):
    gate = sigmoid(gate_act)
    gate_grad = hidden_grad * up_act * gate * (1.0 + gate_act * (1.0 - gate))
    return gate_grad.astype(jnp.bfloat16), (hidden_grad * gate_act * gate).astype(jnp.bfloat16)


def dot32(left, right, dims=(((1,), (0,)), ((), ()))):
    return lax.dot_general(left, right, dims, preferred_element_type=jnp.float32)


def norm_of(rows):
    return jnp.sqrt(jnp.sum(rows * rows, axis=-1) + eps)


def swap(x, axis, difference):
    pairs = [(i, i ^ difference) for i in range(lax.axis_size(axis))]
    return lax.ppermute(x, axis, pairs)


def swap_core(x):
    return swap(x, "fsdp", 1)


def gather_chips(x):
    chips = lax.axis_size("fsdp") // 2
    return jnp.concatenate([x] + [swap(x, "fsdp", 2 * j) for j in range(1, chips)], axis=0)


def gather_dp(x):
    return jnp.concatenate([x] + [swap(x, "dp", j) for j in range(1, lax.axis_size("dp"))], axis=0)


def gather_core(x):
    return jnp.concatenate([x, swap_core(x)], axis=0)


def add_up(pieces):
    total = pieces[0].astype(jnp.float32)
    for piece in pieces[1:]:
        total = total + piece.astype(jnp.float32)
    return total


def sum_core(x):
    rows = x.shape[0] // 2
    return add_up([x[:rows], swap_core(x[rows:])])


def sum_over(x, axis, parts, unit):
    rows = x.shape[0] // parts
    return add_up(
        [x[:rows]]
        + [swap(x[j * rows : (j + 1) * rows], axis, j * unit) for j in range(1, parts)]
    )


def sum_chips(x):
    return sum_over(x, "fsdp", lax.axis_size("fsdp") // 2, 2)


def sum_dp(x):
    return sum_over(x, "dp", lax.axis_size("dp"), 1)


def relative_order(mine, blocks, block_rows):
    rows = blocks * block_rows
    place = lax.broadcasted_iota(jnp.int32, (rows, rows), 0)
    block, row = place // block_rows, place % block_rows
    core, chip = block // (blocks // 2), block % (blocks // 2)
    source = jnp.bitwise_xor(mine[:, None], 2 * chip + core) * block_rows + row
    return (source == lax.broadcasted_iota(jnp.int32, (rows, rows), 1)).astype(jnp.bfloat16)


def use_counts(slots, row_table, count_table, shard, shard_rows):
    devices, queries, negatives = slots.shape
    slot_cap = row_table.shape[1]
    slot = lax.broadcasted_iota(jnp.int32, (1, 1, 1, slot_cap), 3) + shard[:, None, None, None] * slot_cap
    asked = jnp.sum((slots[..., None] == slot).astype(jnp.float32), axis=2)
    live = lax.broadcasted_iota(jnp.int32, (devices, 1, slot_cap), 2) < count_table[:, :, None]
    used = jnp.where(live, asked, 0.0)
    dead = jnp.sum(asked - used, axis=-1).reshape(devices * queries)
    row = lax.broadcasted_iota(jnp.int32, (1, 1, shard_rows), 2)
    picks = (row_table[:, :, None] == row).astype(jnp.bfloat16)
    counts = lax.dot_general(
        used.astype(jnp.bfloat16),
        picks,
        (((2,), (1,)), ((0,), (0,))),
        preferred_element_type=jnp.float32,
    )
    return counts.reshape(devices * queries, shard_rows), dead


in_vmem = pl.BlockSpec(memory_space=pltpu.VMEM)
in_smem = pl.BlockSpec(memory_space=pltpu.SMEM)
in_hbm = pl.BlockSpec(memory_space=pltpu.HBM)
mib = 2**20


def held(x):
    return pltpu.with_memory_space_constraint(x, pltpu.VMEM)


def in_place(x):
    return pltpu.with_memory_space_constraint(x, pltpu.HBM)


def shape_of(shape, dtype=jnp.bfloat16):
    return jax.ShapeDtypeStruct(shape, dtype)


def kernel_call(body, in_specs, out_shape, limit, scratch=()):
    outs = out_shape if isinstance(out_shape, (list, tuple)) else [out_shape]
    specs = [in_vmem] * len(outs)
    return pl.pallas_call(
        body,
        in_specs=in_specs,
        out_specs=specs if isinstance(out_shape, (list, tuple)) else specs[0],
        out_shape=out_shape,
        scratch_shapes=list(scratch),
        compiler_params=pltpu.CompilerParams(vmem_limit_bytes=limit * mib),
    )


def together(*arrays):
    return lax.optimization_barrier(arrays)


def row_copies(order_ref, wanted, sources, held_ref, sems):
    depth = held_ref.shape[2]
    groups = []
    for n, j in enumerate(wanted):
        at = pl.ds(pl.multiple_of(order_ref[j] * depth, depth), depth)
        groups.append(
            [
                pltpu.make_async_copy(source.at[at], held_ref.at[k, n], sems.at[k, n])
                for k, source in enumerate(sources)
            ]
        )
    return groups


def in_turn(groups, ahead):
    for group in groups[:ahead]:
        for copy in group:
            copy.start()
    for n, group in enumerate(groups):
        for copy in group:
            copy.wait()
        for copy in groups[n + ahead] if n + ahead < len(groups) else []:
            copy.start()
        yield n


def forward_part(order, pieces, wanted, rows, gate_weight, up_weight, *totals):
    depth, units = pieces.shape[2], gate_weight.shape[1]
    begun = len(totals)

    def body(order_ref, x_ref, gate_ref, up_ref, *refs):
        starts, outs, (held_ref, sems) = refs[:begun], refs[begun:-2], refs[-2:]
        copies = row_copies(order_ref, wanted, (gate_ref, up_ref), held_ref, sems)
        for n in in_turn(copies, 3):
            for k, out in enumerate(outs):
                term = dot32(x_ref[wanted[n], :rows], held_ref[k, n])
                if n:
                    term = term + out[...]
                elif begun:
                    term = term + starts[k][...]
                out[...] = term

    return kernel_call(
        body,
        [in_smem, in_vmem, in_hbm, in_hbm] + [in_vmem] * begun,
        [shape_of((rows, units), jnp.float32)] * 2,
        18,
        [
            pltpu.VMEM((2, len(wanted), depth, units), gate_weight.dtype),
            pltpu.SemaphoreType.DMA((2, len(wanted))),
        ],
    )(order, pieces, in_place(gate_weight), in_place(up_weight), *totals)


def forward_rest(
    order, pieces, gate_part, up_part, gate_weight, up_weight, down_weight, to_relative, extra
):
    parts, _, depth = pieces.shape
    rows, units = gate_part.shape
    width = down_weight.shape[1]
    chunk = width // 8
    wanted = range(parts, 2 * parts)

    def body(
        order_ref, x_ref, gate_in, up_in, gate_ref, up_ref, down_ref, one_hot, extra_ref,
        gate_out, up_out, own_out, other_out, held_ref, down_held, totals, sems, down_sems,
    ):
        copies = row_copies(order_ref, wanted, (gate_ref, up_ref), held_ref, sems)
        for i in range(8):
            at = pl.ds(i * chunk, chunk)
            copies.append(
                [pltpu.make_async_copy(down_ref.at[:, at], down_held.at[i], down_sems.at[i])]
            )
        hidden = None
        for n in in_turn(copies, 4):
            if n < parts:
                for k, start in enumerate((gate_in, up_in)):
                    term = dot32(x_ref[n, :rows], held_ref[k, n])
                    totals[k] = term + (totals[k] if n else start[...])
                continue
            if hidden is None:
                gate, up = totals[0], totals[1]
                gate_out[:rows] = gate.astype(jnp.bfloat16)
                gate_out[rows:] = extra_ref[...]
                up_out[:rows] = up.astype(jnp.bfloat16)
                up_out[rows:] = extra_ref[...]
                hidden = (gate * sigmoid(gate) * up).astype(jnp.bfloat16)
                hidden = dot32(one_hot[...], hidden).astype(jnp.bfloat16)
            at = pl.ds((n - parts) * chunk, chunk)
            total = dot32(hidden, down_held[n - parts])
            own_out[:, at] = total[: rows // 2].astype(jnp.bfloat16)
            other_out[:, at] = total[rows // 2 :].astype(jnp.bfloat16)

    return kernel_call(
        body,
        [in_smem] + [in_vmem] * 3 + [in_hbm] * 3 + [in_vmem] * 2,
        [shape_of((rows + extra.shape[0], units))] * 2 + [shape_of((rows // 2, width))] * 2,
        36,
        [
            pltpu.VMEM((2, parts, depth, units), gate_weight.dtype),
            pltpu.VMEM((8, units, chunk), down_weight.dtype),
            pltpu.VMEM((2, rows, units), jnp.float32),
            pltpu.SemaphoreType.DMA((2, parts)),
            pltpu.SemaphoreType.DMA((8,)),
        ],
    )(
        order,
        pieces,
        gate_part,
        up_part,
        in_place(gate_weight),
        in_place(up_weight),
        in_place(down_weight),
        to_relative,
        extra,
    )


def input_blocks(place, order, first, second, rows, parts):
    half, _, depth = first.shape
    share = 2 * half // parts

    def body(place_ref, order_ref, first_ref, second_ref, *refs):
        outs, whole = refs[:parts], refs[parts]
        for j in range(2 * half):
            at = order_ref[j]
            to = pl.ds(pl.multiple_of((at % share) * depth, depth), depth)
            piece = first_ref[j, :rows] if j < half else second_ref[j - half, :rows]
            whole[at // share ^ place_ref[0], :, to] = piece
        for k, out in enumerate(outs):
            out[...] = whole[k]

    return kernel_call(
        body,
        [in_smem, in_smem, in_vmem, in_vmem],
        [shape_of((rows, share * depth))] * parts,
        4,
        [pltpu.VMEM((parts, rows, share * depth), first.dtype)],
    )(place, order, first, second)


def score_kernel(states, index_parts, inverse_norm, counts, dead, pad):
    pieces = len(states)
    rows, width = states[0].shape
    shard = index_parts[0].shape[0]
    chunk = width // 8

    def body(*refs):
        state_refs, refs = refs[:pieces], refs[pieces:]
        sources, (inverse_ref, counts_ref, dead_ref) = refs[:2], refs[2:5]
        outs, (index_held, sems) = refs[5:-2], refs[-2:]
        copies = [
            pltpu.make_async_copy(source, index_held.at[k], sems.at[k])
            for k, source in enumerate(sources)
        ]
        for copy in copies:
            copy.start()
        block = jnp.concatenate([r[...] for r in state_refs], axis=0)
        values = block.astype(jnp.float32)
        state_scale = inverse_temp / jnp.sqrt(jnp.sum(values * values, axis=1, keepdims=True) + eps)
        total = dead_ref[...]
        coeffs = []
        for k, copy in enumerate(copies):
            copy.wait()
            inverse = inverse_ref[:, k * shard : (k + 1) * shard]
            raw = dot32(block, index_held[k], contract_last)
            weights = counts_ref[:, k * shard : (k + 1) * shard] * jnp.exp(raw * state_scale * inverse)
            total = total + jnp.sum(weights, axis=1, keepdims=True)
            coeffs.append((weights * inverse).astype(jnp.bfloat16))
        column = lax.broadcasted_iota(jnp.int32, (pieces * rows, pad), 1)
        last = jnp.where(column == 0, total, 0.0).astype(jnp.bfloat16)
        for p in range(pieces):
            outs[p][:, width:] = last[p * rows : (p + 1) * rows]
        for i in range(width // chunk):
            at = pl.ds(i * chunk, chunk)
            pull = dot32(coeffs[0], index_held[0, :, at]) + dot32(coeffs[1], index_held[1, :, at])
            for p in range(pieces):
                outs[p][:, at] = pull[p * rows : (p + 1) * rows].astype(jnp.bfloat16)

    return kernel_call(
        body,
        [in_vmem] * pieces + [in_hbm] * 2 + [in_vmem] * 3,
        [shape_of((rows, width + pad))] * pieces,
        20,
        [
            pltpu.VMEM((2, shard, width), index_parts[0].dtype),
            pltpu.SemaphoreType.DMA((2,)),
        ],
    )(*states, *[in_place(x) for x in index_parts], inverse_norm, counts, dead)


def backward_hidden(order, own_rows, other_rows, down_weight, gate_act, up_act, to_relative, parts):
    half, width = own_rows.shape
    rows, units = 2 * half, down_weight.shape[0]
    part = width // parts
    chunk = 256 if units % 256 == 0 else units
    chunks = units // chunk
    slots = min(chunks, 5)

    def body(order_ref, own_ref, other_ref, down_ref, gate_ref, up_ref, one_hot, *refs):
        gate_out, up_out = refs[:2]
        outs, (grad_ref, turned_ref, held_ref, sems) = refs[2:-4], refs[-4:]
        spans = [pl.ds(i * chunk, chunk) for i in range(chunks)]
        copies = [
            pltpu.make_async_copy(down_ref.at[at], held_ref.at[i % slots], sems.at[i % slots])
            for i, at in enumerate(spans)
        ]
        for copy in copies[: max(slots - 1, 1)]:
            copy.start()
        grad = jnp.concatenate([own_ref[...], other_ref[...]], axis=0)
        grad_ref[...] = dot32(one_hot[...], grad, contract_first).astype(jnp.bfloat16)
        turned_ref[...] = grad_ref[...].T
        for k, out in enumerate(outs):
            out[:, units:] = grad_ref[:, pl.ds(pl.multiple_of(order_ref[k] * part, part), part)]
        for i, at in enumerate(spans):
            copies[i].wait()
            if i + slots - 1 < chunks and slots > 1:
                copies[i + slots - 1].start()
            hidden_grad = dot32(held_ref[i % slots], turned_ref[...]).T
            for out in outs:
                out[:, at] = hidden_grad.astype(jnp.bfloat16)
            gate_out[:, at], up_out[:, at] = activation_grads(
                hidden_grad,
                gate_ref[:rows, at].astype(jnp.float32),
                up_ref[:rows, at].astype(jnp.float32),
            )

    outs = kernel_call(
        body,
        [in_smem, in_vmem, in_vmem, in_hbm, in_vmem, in_vmem, in_vmem],
        [shape_of((rows, units))] * 2 + [shape_of((rows, units + part))] * parts,
        16,
        [
            pltpu.VMEM((rows, width), jnp.bfloat16),
            pltpu.VMEM((width, rows), jnp.bfloat16),
            pltpu.VMEM((slots, chunk, width), down_weight.dtype),
            pltpu.SemaphoreType.DMA((slots,)),
        ],
    )(order, own_rows, other_rows, in_place(down_weight), gate_act, up_act, to_relative)
    return outs[0], outs[1], outs[2:]


def backward_input(order, gate_grad, up_grad, gate_weight, up_weight):
    rows, units = gate_grad.shape
    width = gate_weight.shape[0]
    blocks = order.shape[0]
    depth = width // blocks
    half = blocks // 2
    slots = 4

    def body(order_ref, gate_grad_ref, up_grad_ref, gate_ref, up_ref, own_out, other_out, held_ref, sems):
        def copies_of(n):
            at = pl.ds(pl.multiple_of(order_ref[n] * depth, depth), depth)
            return [
                pltpu.make_async_copy(source.at[at], held_ref.at[k, n % slots], sems.at[k, n % slots])
                for k, source in enumerate((gate_ref, up_ref))
            ]

        for n in range(slots - 1):
            for copy in copies_of(n):
                copy.start()
        for n in range(blocks):
            for copy in copies_of(n):
                copy.wait()
            if n + slots - 1 < blocks:
                for copy in copies_of(n + slots - 1):
                    copy.start()
            block = dot32(gate_grad_ref[...], held_ref[0, n % slots], contract_last) + dot32(
                up_grad_ref[...], held_ref[1, n % slots], contract_last
            )
            out = own_out if n < half else other_out
            out[n % half] = block.astype(jnp.bfloat16)

    return kernel_call(
        body,
        [in_smem, in_vmem, in_vmem, in_hbm, in_hbm],
        [shape_of((half, rows, depth))] * 2,
        18,
        [
            pltpu.VMEM((2, slots, depth, units), gate_weight.dtype),
            pltpu.SemaphoreType.DMA((2, slots)),
        ],
    )(order, gate_grad, up_grad, in_place(gate_weight), in_place(up_weight))


def weight_grads(input_columns, grads, gate_acts, up_acts):
    groups = len(grads)
    rows, units = grads[0].shape[0], gate_acts[0].shape[1]
    width = input_columns[0].shape[1]
    chunk = 256 if units % 256 == 0 else units
    chunks = units // chunk

    def body(*refs):
        columns, refs = refs[:groups], refs[groups:]
        (gate_out, up_out, turned, made, sems), refs = refs[3 * groups :], refs[: 3 * groups]
        turned[...] = jnp.concatenate([r[...] for r in columns], axis=0).T
        copies = []
        for i in range(chunks):
            at = pl.ds(i * chunk, chunk)
            hidden_grad, gate, up = (
                jnp.concatenate([r[:rows, at] for r in refs[k * groups : (k + 1) * groups]], axis=0)
                for k in range(3)
            )
            both = activation_grads(
                hidden_grad.astype(jnp.float32), gate.astype(jnp.float32), up.astype(jnp.float32)
            )
            for k, out in enumerate((gate_out, up_out)):
                made[k, i] = dot32(turned[...], both[k]).astype(jnp.bfloat16)
                copies.append(
                    pltpu.make_async_copy(made.at[k, i], out.at[:, at], sems.at[k, i])
                )
                copies[-1].start()
        for copy in copies:
            copy.wait()

    return pl.pallas_call(
        body,
        in_specs=[in_vmem] * (4 * groups),
        out_specs=[pl.BlockSpec(memory_space=pl.ANY)] * 2,
        out_shape=[shape_of((width, units))] * 2,
        scratch_shapes=[
            pltpu.VMEM((width, groups * rows), jnp.bfloat16),
            pltpu.VMEM((2, chunks, width, chunk), jnp.bfloat16),
            pltpu.SemaphoreType.DMA((2, chunks)),
        ],
        compiler_params=pltpu.CompilerParams(vmem_limit_bytes=18 * mib),
    )(*input_columns, *grads, *gate_acts, *up_acts)


def down_grads(grads, gate_acts, up_acts):
    groups = len(grads)
    rows, units = grads[0].shape[0], gate_acts[0].shape[1]
    width = grads[0].shape[1] - units
    chunk = 256 if units % 256 == 0 else units
    chunks = units // chunk

    def body(*refs):
        (out, made, sems), refs = refs[3 * groups :], refs[: 3 * groups]
        head_grad = jnp.concatenate([r[:, units:] for r in refs[:groups]], axis=0)
        copies = []
        for i in range(chunks):
            at = pl.ds(i * chunk, chunk)
            gate, up = (
                jnp.concatenate([r[:rows, at] for r in refs[k * groups : (k + 1) * groups]], axis=0)
                for k in (1, 2)
            )
            gate, up = gate.astype(jnp.float32), up.astype(jnp.float32)
            hidden = (gate * sigmoid(gate) * up).astype(jnp.bfloat16)
            made[i] = dot32(hidden, head_grad, contract_first).astype(jnp.bfloat16)
            copies.append(pltpu.make_async_copy(made.at[i], out.at[at], sems.at[i]))
            copies[-1].start()
        for copy in copies:
            copy.wait()

    return pl.pallas_call(
        body,
        in_specs=[in_vmem] * (3 * groups),
        out_specs=pl.BlockSpec(memory_space=pl.ANY),
        out_shape=shape_of((units, width)),
        scratch_shapes=[
            pltpu.VMEM((chunks, chunk, width), jnp.bfloat16),
            pltpu.SemaphoreType.DMA((chunks,)),
        ],
        compiler_params=pltpu.CompilerParams(vmem_limit_bytes=14 * mib),
    )(*grads, *gate_acts, *up_acts)


def shards(
    mlp_input,
    residual_in,
    gate_weight,
    up_weight,
    down_weight,
    span_index,
    positive_keys,
    request_rows,
    request_counts,
    negative_slots,
):
    dp_count = lax.axis_size("dp")
    fsdp_count = lax.axis_size("fsdp")
    chips = fsdp_count // 2
    place = jnp.stack([lax.axis_index("dp"), lax.axis_index("fsdp")])
    my_dp, my_fsdp = place[:1], place[1:]
    me = my_dp * fsdp_count + my_fsdp
    width = span_index.shape[1]
    own_queries = negative_slots.shape[0]
    group_rows = mlp_input.shape[0]
    j = jnp.arange(fsdp_count, dtype=jnp.int32)
    fsdp_order = jnp.bitwise_xor(my_fsdp, 2 * (j % chips) + j // chips).astype(jnp.int32)
    dp_order = jnp.bitwise_xor(my_dp, jnp.arange(dp_count, dtype=jnp.int32)).astype(jnp.int32)
    to_relative = relative_order(my_fsdp, fsdp_count, own_queries)
    j = jnp.arange(dp_count * chips, dtype=jnp.int32)
    asker = jnp.bitwise_xor(my_dp, j // chips) * fsdp_count + jnp.bitwise_xor(
        my_fsdp, 2 * (j % chips)
    )
    both = jnp.concatenate([me, jnp.bitwise_xor(me, 1)])
    place, fsdp_order, dp_order, to_relative, asker, both = together(
        place, fsdp_order, dp_order, to_relative, asker, both
    )

    slot_cap, negatives = request_rows.shape[2], negative_slots.shape[1]
    slots = jnp.concatenate([negative_slots // slot_cap, negative_slots % slot_cap], axis=1)
    slots = jnp.pad(slots, ((0, 0), (0, mlp_input.shape[1] - 2 * negatives)))
    message = jnp.concatenate([mlp_input, slots.astype(jnp.bfloat16)], axis=0)
    parts = forward_part(fsdp_order, message[None], (0,), group_rows, gate_weight, up_weight)
    first, *parts = together(gather_chips(message[None]), *parts)
    second = swap_core(first)
    gate_part, up_part = forward_part(
        fsdp_order, first, tuple(range(1, chips)), group_rows, gate_weight, up_weight, *parts
    )
    tables = jnp.concatenate([request_rows[:, 0, :], request_counts], axis=1)[None]
    gate_part, up_part, second, span_later, tables = together(
        gate_part, up_part, second, span_index, gather_core(tables)
    )
    units = up_weight.shape[1]
    bands = units // (2 * negatives)
    extra = [first[c, group_rows:, : 2 * negatives] for c in range(chips)]
    extra = [jnp.concatenate(extra[i : i + bands], axis=1) for i in range(0, chips, bands)]
    extra = [jnp.pad(x, ((0, 0), (0, units - x.shape[1]))) for x in extra]
    extra = jnp.concatenate(extra, axis=0)
    other_index = swap_core(span_later)
    gate_act, up_act, own_part, other_part = forward_rest(
        fsdp_order,
        second,
        gate_part,
        up_part,
        gate_weight,
        up_weight,
        down_weight,
        to_relative,
        extra,
    )

    near, far = 1, dp_count // 2
    own_part, other_part, other_index = together(own_part, other_part, other_index)
    own_part, received, gate_act, up_act, span_later, tables = together(
        own_part, swap_core(other_part), gate_act, up_act, span_later, tables
    )
    branch = add_up([own_part, received]).astype(jnp.bfloat16)

    tables = jnp.take(tables, asker, axis=1)
    row_tables, count_tables = tables[..., :-1], tables[..., -1:]
    top_state, gate_near, up_far, own_norm, span_later, other_index, row_tables, count_tables = together(
        sum_chips(branch) + residual_in.astype(jnp.float32),
        swap(gate_act, "dp", near),
        swap(up_act, "dp", far),
        norm_of(span_later.astype(jnp.float32)),
        span_later,
        other_index,
        row_tables,
        count_tables,
    )
    row_norm = norm_of(top_state)
    unit_rows = top_state / row_norm[:, None]

    states, last_slots, other_norm, span_later, other_index, row_tables, count_tables, positive_keys, both = together(
        gather_chips(top_state.astype(jnp.bfloat16)),
        swap(gate_near[group_rows:], "dp", far),
        swap_core(own_norm),
        span_later,
        other_index,
        row_tables,
        count_tables,
        positive_keys,
        both,
    )
    index_norm = jnp.concatenate([own_norm, other_norm], axis=0)
    slots = [x[group_rows:] for x in (gate_act, gate_near, up_far)] + [last_slots]
    slots = jnp.stack(slots).astype(jnp.int32)
    slots = [
        slots[
            :,
            c // bands * own_queries : (c // bands + 1) * own_queries,
            c % bands * 2 * negatives : (c % bands + 1) * 2 * negatives,
        ]
        for c in range(chips)
    ]
    slots = jnp.stack(slots, axis=1).reshape(dp_count * chips, own_queries, 2 * negatives)
    slots = slots[..., :negatives] * slot_cap + slots[..., negatives:]
    counts, dead = [], 0.0
    for k in range(2):
        shard_counts, shard_dead = use_counts(
            slots,
            row_tables[k],
            count_tables[k],
            both[k : k + 1],
            span_index.shape[0],
        )
        counts.append(shard_counts)
        dead = dead + shard_dead
    counts = jnp.concatenate(counts, axis=1)
    states = [states] + [swap(states, "dp", k) for k in range(1, dp_count)]
    counts, dead, *states = together(counts, dead, *states)
    index_parts = [span_later, other_index]
    pulls = score_kernel(
        states, index_parts, (1.0 / index_norm)[None, :], counts, dead[:, None], 128
    )

    sums = add_up([pulls[0]] + [swap(pulls[k], "dp", k) for k in range(1, dp_count)])
    sums, gate_act, up_act, first, second = together(
        sums.astype(jnp.bfloat16), gate_act, up_act, first, second
    )
    sums, gate_far, up_near, *blocks = together(
        sum_chips(sums),
        swap(gate_act, "dp", far),
        swap(up_act, "dp", near),
        *input_blocks(place, fsdp_order, first, second, group_rows, dp_count),
    )
    negative_total = sums[:, width]
    positive_rows = positive_keys.astype(jnp.float32)
    positive_unit = positive_rows / norm_of(positive_rows)[:, None]
    positive_score = inverse_temp * jnp.sum(unit_rows * positive_unit, axis=-1)
    exp_total = jnp.exp(positive_score) + negative_total
    query_loss = jnp.log(exp_total) - positive_score
    pull = (sums[:, :width] - negative_total[:, None] * positive_unit) / exp_total[:, None]
    inner = jnp.sum(pull * unit_rows, axis=-1)
    head_grad = (
        inverse_temp * (pull - inner[:, None] * unit_rows) / row_norm[:, None]
    ).astype(jnp.bfloat16)

    own_rows, block_near, block_far, gate_near, up_far = together(
        gather_chips(head_grad),
        swap(blocks[near], "dp", near),
        swap(blocks[far], "dp", far),
        gate_near,
        up_far,
    )
    gate_last, up_last = swap(gate_near, "dp", far), swap(up_far, "dp", near)
    other_rows = swap_core(own_rows)
    own_gate_grad, own_up_grad, grads = backward_hidden(
        dp_order, own_rows, other_rows, down_weight, gate_act, up_act, to_relative, dp_count
    )
    own_gate_grad, own_up_grad, gate_last, up_last, block_last, *grads = together(
        own_gate_grad,
        own_up_grad,
        gate_last,
        up_last,
        swap(blocks[near + far], "dp", near + far),
        *grads,
    )
    blocks = [blocks[0], block_near, block_far, block_last]
    gates = [gate_act, gate_near, gate_far, gate_last]
    ups = [up_act, up_near, up_far, up_last]
    grads = [grads[0]] + [swap(grads[k], "dp", k) for k in range(1, dp_count)]
    own_blocks, other_blocks = backward_input(
        fsdp_order, own_gate_grad, own_up_grad, gate_weight, up_weight
    )
    own_blocks, other_blocks, *grads = together(own_blocks, other_blocks, *grads)
    received = swap_core(other_blocks)
    down_grad = down_grads(grads, gates, ups)
    own_blocks, received, down_grad = together(own_blocks, received, down_grad)
    blocks_sum = add_up([own_blocks, received]).astype(jnp.bfloat16)
    input_grad = sum_chips(blocks_sum)[0].astype(jnp.bfloat16)
    gate_grad, up_grad = weight_grads(blocks, grads, gates, ups)
    return (query_loss, input_grad, gate_grad, up_grad, down_grad)


def solution(mesh):
    return jax.shard_map(
        shards,
        mesh=mesh,
        in_specs=(
            P("dp", "fsdp"),
            P(("dp", "fsdp"), None),
            P(None, "fsdp"),
            P(None, "fsdp"),
            P("fsdp", None),
            P(("dp", "fsdp"), None),
            P(("dp", "fsdp"), None),
            P(None, ("dp", "fsdp"), None),
            P(None, ("dp", "fsdp")),
            P(("dp", "fsdp"), None),
        ),
        out_specs=(
            P(("dp", "fsdp")),
            P("dp", "fsdp"),
            P("dp", "fsdp"),
            P("dp", "fsdp"),
            P("fsdp", "dp"),
        ),
        check_vma=False,
    )
```

```python
import jax
import jax.numpy as jnp
from jax import lax
from jax.experimental import pallas as pl
from jax.experimental.pallas import tpu as pltpu
from jax.sharding import PartitionSpec as P

inverse_temp = 50.0
eps = 1e-06
contract_first = (((0,), (0,)), ((), ()))
contract_last = (((1,), (1,)), ((), ()))
every = ("dp", "fsdp")


def sigmoid(v):
    return 1.0 / (1.0 + jnp.exp(-v))


def activation_grads(hidden_grad, gate_act, up_act):
    gate = sigmoid(gate_act)
    gate_grad = hidden_grad * up_act * gate * (1.0 + gate_act * (1.0 - gate))
    return gate_grad.astype(jnp.bfloat16), (hidden_grad * gate_act * gate).astype(jnp.bfloat16)


def dot32(left, right, dims=(((1,), (0,)), ((), ()))):
    return lax.dot_general(left, right, dims, preferred_element_type=jnp.float32)


def norm_of(rows):
    return jnp.sqrt(jnp.sum(rows * rows, axis=-1) + eps)


def swap(x, axis, difference):
    pairs = [(i, i ^ difference) for i in range(lax.axis_size(axis))]
    return lax.ppermute(x, axis, pairs)


def swap_core(x):
    return swap(x, "fsdp", 1)


def gather_chips(x):
    chips = lax.axis_size("fsdp") // 2
    return jnp.concatenate([x] + [swap(x, "fsdp", 2 * j) for j in range(1, chips)], axis=0)


def gather_dp(x):
    return jnp.concatenate([x] + [swap(x, "dp", j) for j in range(1, lax.axis_size("dp"))], axis=0)


def gather_core(x):
    return jnp.concatenate([x, swap_core(x)], axis=0)


def add_up(pieces):
    total = pieces[0].astype(jnp.float32)
    for piece in pieces[1:]:
        total = total + piece.astype(jnp.float32)
    return total


def sum_core(x):
    rows = x.shape[0] // 2
    return add_up([x[:rows], swap_core(x[rows:])])


def sum_over(x, axis, parts, unit):
    rows = x.shape[0] // parts
    return add_up(
        [x[:rows]]
        + [swap(x[j * rows : (j + 1) * rows], axis, j * unit) for j in range(1, parts)]
    )


def sum_chips(x):
    return sum_over(x, "fsdp", lax.axis_size("fsdp") // 2, 2)


def sum_dp(x):
    return sum_over(x, "dp", lax.axis_size("dp"), 1)


def relative_order(mine, blocks, block_rows):
    rows = blocks * block_rows
    place = lax.broadcasted_iota(jnp.int32, (rows, rows), 0)
    block, row = place // block_rows, place % block_rows
    core, chip = block // (blocks // 2), block % (blocks // 2)
    source = jnp.bitwise_xor(mine[:, None], 2 * chip + core) * block_rows + row
    return (source == lax.broadcasted_iota(jnp.int32, (rows, rows), 1)).astype(jnp.bfloat16)


def use_counts(slots, row_table, count_table, shard, shard_rows):
    devices, queries, negatives = slots.shape
    slot_cap = row_table.shape[1]
    slot = lax.broadcasted_iota(jnp.int32, (1, 1, 1, slot_cap), 3) + shard[:, None, None, None] * slot_cap
    asked = jnp.sum((slots[..., None] == slot).astype(jnp.float32), axis=2)
    live = lax.broadcasted_iota(jnp.int32, (devices, 1, slot_cap), 2) < count_table[:, :, None]
    used = jnp.where(live, asked, 0.0)
    dead = jnp.sum(asked - used, axis=-1).reshape(devices * queries)
    row = lax.broadcasted_iota(jnp.int32, (1, 1, shard_rows), 2)
    picks = (row_table[:, :, None] == row).astype(jnp.bfloat16)
    counts = lax.dot_general(
        used.astype(jnp.bfloat16),
        picks,
        (((2,), (1,)), ((0,), (0,))),
        preferred_element_type=jnp.float32,
    )
    return counts.reshape(devices * queries, shard_rows), dead


in_vmem = pl.BlockSpec(memory_space=pltpu.VMEM)
in_smem = pl.BlockSpec(memory_space=pltpu.SMEM)
in_hbm = pl.BlockSpec(memory_space=pltpu.HBM)
mib = 2**20


def held(x):
    return pltpu.with_memory_space_constraint(x, pltpu.VMEM)


def in_place(x):
    return pltpu.with_memory_space_constraint(x, pltpu.HBM)


def shape_of(shape, dtype=jnp.bfloat16):
    return jax.ShapeDtypeStruct(shape, dtype)


def kernel_call(body, in_specs, out_shape, limit, scratch=()):
    outs = out_shape if isinstance(out_shape, (list, tuple)) else [out_shape]
    specs = [in_vmem] * len(outs)
    return pl.pallas_call(
        body,
        in_specs=in_specs,
        out_specs=specs if isinstance(out_shape, (list, tuple)) else specs[0],
        out_shape=out_shape,
        scratch_shapes=list(scratch),
        compiler_params=pltpu.CompilerParams(vmem_limit_bytes=limit * mib),
    )


def together(*arrays):
    return lax.optimization_barrier(arrays)


def row_copies(order_ref, wanted, sources, held_ref, sems):
    depth = held_ref.shape[2]
    groups = []
    for n, j in enumerate(wanted):
        at = pl.ds(pl.multiple_of(order_ref[j] * depth, depth), depth)
        groups.append(
            [
                pltpu.make_async_copy(source.at[at], held_ref.at[k, n], sems.at[k, n])
                for k, source in enumerate(sources)
            ]
        )
    return groups


def in_turn(groups, ahead):
    for group in groups[:ahead]:
        for copy in group:
            copy.start()
    for n, group in enumerate(groups):
        for copy in group:
            copy.wait()
        for copy in groups[n + ahead] if n + ahead < len(groups) else []:
            copy.start()
        yield n


def forward_part(order, pieces, wanted, rows, gate_weight, up_weight, *totals):
    depth, units = pieces.shape[2], gate_weight.shape[1]
    begun = len(totals)

    def body(order_ref, x_ref, gate_ref, up_ref, *refs):
        starts, outs, (held_ref, sems) = refs[:begun], refs[begun:-2], refs[-2:]
        copies = row_copies(order_ref, wanted, (gate_ref, up_ref), held_ref, sems)
        for n in in_turn(copies, 3):
            for k, out in enumerate(outs):
                term = dot32(x_ref[wanted[n], :rows], held_ref[k, n])
                if n:
                    term = term + out[...]
                elif begun:
                    term = term + starts[k][...]
                out[...] = term

    return kernel_call(
        body,
        [in_smem, in_vmem, in_hbm, in_hbm] + [in_vmem] * begun,
        [shape_of((rows, units), jnp.float32)] * 2,
        18,
        [
            pltpu.VMEM((2, len(wanted), depth, units), gate_weight.dtype),
            pltpu.SemaphoreType.DMA((2, len(wanted))),
        ],
    )(order, pieces, in_place(gate_weight), in_place(up_weight), *totals)


def forward_rest(
    order, pieces, gate_part, up_part, gate_weight, up_weight, down_weight, to_relative, extra
):
    parts, _, depth = pieces.shape
    rows, units = gate_part.shape
    width = down_weight.shape[1]
    chunk = width // 8
    wanted = range(parts, 2 * parts)

    def body(
        order_ref, x_ref, gate_in, up_in, gate_ref, up_ref, down_ref, one_hot, extra_ref,
        gate_out, up_out, own_out, other_out, held_ref, down_held, totals, sems, down_sems,
    ):
        copies = row_copies(order_ref, wanted, (gate_ref, up_ref), held_ref, sems)
        for i in range(8):
            at = pl.ds(i * chunk, chunk)
            copies.append(
                [pltpu.make_async_copy(down_ref.at[:, at], down_held.at[i], down_sems.at[i])]
            )
        hidden = None
        for n in in_turn(copies, 7):
            if n < parts:
                for k, start in enumerate((gate_in, up_in)):
                    term = dot32(x_ref[n, :rows], held_ref[k, n])
                    totals[k] = term + (totals[k] if n else start[...])
                continue
            if hidden is None:
                gate, up = totals[0], totals[1]
                gate_out[:rows] = gate.astype(jnp.bfloat16)
                gate_out[rows:] = extra_ref[...]
                up_out[:rows] = up.astype(jnp.bfloat16)
                up_out[rows:] = extra_ref[...]
                hidden = (gate * sigmoid(gate) * up).astype(jnp.bfloat16)
                hidden = dot32(one_hot[...], hidden).astype(jnp.bfloat16)
            at = pl.ds((n - parts) * chunk, chunk)
            total = dot32(hidden, down_held[n - parts])
            own_out[:, at] = total[: rows // 2].astype(jnp.bfloat16)
            other_out[:, at] = total[rows // 2 :].astype(jnp.bfloat16)

    return kernel_call(
        body,
        [in_smem] + [in_vmem] * 3 + [in_hbm] * 3 + [in_vmem] * 2,
        [shape_of((rows + extra.shape[0], units))] * 2 + [shape_of((rows // 2, width))] * 2,
        36,
        [
            pltpu.VMEM((2, parts, depth, units), gate_weight.dtype),
            pltpu.VMEM((8, units, chunk), down_weight.dtype),
            pltpu.VMEM((2, rows, units), jnp.float32),
            pltpu.SemaphoreType.DMA((2, parts)),
            pltpu.SemaphoreType.DMA((8,)),
        ],
    )(
        order,
        pieces,
        gate_part,
        up_part,
        in_place(gate_weight),
        in_place(up_weight),
        in_place(down_weight),
        to_relative,
        extra,
    )


def input_blocks(place, order, first, second, rows, parts):
    half, _, depth = first.shape
    share = 2 * half // parts

    def body(place_ref, order_ref, first_ref, second_ref, *refs):
        outs, whole = refs[:parts], refs[parts]
        for j in range(2 * half):
            at = order_ref[j]
            to = pl.ds(pl.multiple_of((at % share) * depth, depth), depth)
            piece = first_ref[j, :rows] if j < half else second_ref[j - half, :rows]
            whole[at // share ^ place_ref[0], :, to] = piece
        for k, out in enumerate(outs):
            out[...] = whole[k]

    return kernel_call(
        body,
        [in_smem, in_smem, in_vmem, in_vmem],
        [shape_of((rows, share * depth))] * parts,
        4,
        [pltpu.VMEM((parts, rows, share * depth), first.dtype)],
    )(place, order, first, second)


def score_kernel(states, index_parts, inverse_norm, counts, dead, pad):
    pieces = len(states)
    rows, width = states[0].shape
    shard = index_parts[0].shape[0]
    chunk = width // 8

    def body(*refs):
        state_refs, refs = refs[:pieces], refs[pieces:]
        sources, (inverse_ref, counts_ref, dead_ref) = refs[:2], refs[2:5]
        outs, (index_held, sems) = refs[5:-2], refs[-2:]
        copies = [
            pltpu.make_async_copy(source, index_held.at[k], sems.at[k])
            for k, source in enumerate(sources)
        ]
        for copy in copies:
            copy.start()
        block = jnp.concatenate([r[...] for r in state_refs], axis=0)
        values = block.astype(jnp.float32)
        state_scale = inverse_temp / jnp.sqrt(jnp.sum(values * values, axis=1, keepdims=True) + eps)
        total = dead_ref[...]
        coeffs = []
        for k, copy in enumerate(copies):
            copy.wait()
            inverse = inverse_ref[:, k * shard : (k + 1) * shard]
            raw = dot32(block, index_held[k], contract_last)
            weights = counts_ref[:, k * shard : (k + 1) * shard] * jnp.exp(raw * state_scale * inverse)
            total = total + jnp.sum(weights, axis=1, keepdims=True)
            coeffs.append((weights * inverse).astype(jnp.bfloat16))
        column = lax.broadcasted_iota(jnp.int32, (pieces * rows, pad), 1)
        last = jnp.where(column == 0, total, 0.0).astype(jnp.bfloat16)
        for p in range(pieces):
            outs[p][:, width:] = last[p * rows : (p + 1) * rows]
        for i in range(width // chunk):
            at = pl.ds(i * chunk, chunk)
            pull = dot32(coeffs[0], index_held[0, :, at]) + dot32(coeffs[1], index_held[1, :, at])
            for p in range(pieces):
                outs[p][:, at] = pull[p * rows : (p + 1) * rows].astype(jnp.bfloat16)

    return kernel_call(
        body,
        [in_vmem] * pieces + [in_hbm] * 2 + [in_vmem] * 3,
        [shape_of((rows, width + pad))] * pieces,
        20,
        [
            pltpu.VMEM((2, shard, width), index_parts[0].dtype),
            pltpu.SemaphoreType.DMA((2,)),
        ],
    )(*states, *[in_place(x) for x in index_parts], inverse_norm, counts, dead)


def backward_hidden(order, own_rows, other_rows, down_weight, gate_act, up_act, to_relative, parts):
    half, width = own_rows.shape
    rows, units = 2 * half, down_weight.shape[0]
    part = width // parts
    chunk = 256 if units % 256 == 0 else units
    chunks = units // chunk
    slots = min(chunks, 5)

    def body(order_ref, own_ref, other_ref, down_ref, gate_ref, up_ref, one_hot, *refs):
        gate_out, up_out = refs[:2]
        outs, (grad_ref, turned_ref, held_ref, sems) = refs[2:-4], refs[-4:]
        spans = [pl.ds(i * chunk, chunk) for i in range(chunks)]
        copies = [
            pltpu.make_async_copy(down_ref.at[at], held_ref.at[i % slots], sems.at[i % slots])
            for i, at in enumerate(spans)
        ]
        for copy in copies[: max(slots - 1, 1)]:
            copy.start()
        grad = jnp.concatenate([own_ref[...], other_ref[...]], axis=0)
        grad_ref[...] = dot32(one_hot[...], grad, contract_first).astype(jnp.bfloat16)
        turned_ref[...] = grad_ref[...].T
        for k, out in enumerate(outs):
            out[:, units:] = grad_ref[:, pl.ds(pl.multiple_of(order_ref[k] * part, part), part)]
        for i, at in enumerate(spans):
            copies[i].wait()
            if i + slots - 1 < chunks and slots > 1:
                copies[i + slots - 1].start()
            hidden_grad = dot32(held_ref[i % slots], turned_ref[...]).T
            for out in outs:
                out[:, at] = hidden_grad.astype(jnp.bfloat16)
            gate_out[:, at], up_out[:, at] = activation_grads(
                hidden_grad,
                gate_ref[:rows, at].astype(jnp.float32),
                up_ref[:rows, at].astype(jnp.float32),
            )

    outs = kernel_call(
        body,
        [in_smem, in_vmem, in_vmem, in_hbm, in_vmem, in_vmem, in_vmem],
        [shape_of((rows, units))] * 2 + [shape_of((rows, units + part))] * parts,
        16,
        [
            pltpu.VMEM((rows, width), jnp.bfloat16),
            pltpu.VMEM((width, rows), jnp.bfloat16),
            pltpu.VMEM((slots, chunk, width), down_weight.dtype),
            pltpu.SemaphoreType.DMA((slots,)),
        ],
    )(order, own_rows, other_rows, in_place(down_weight), gate_act, up_act, to_relative)
    return outs[0], outs[1], outs[2:]


def backward_input(order, gate_grad, up_grad, gate_weight, up_weight):
    rows, units = gate_grad.shape
    width = gate_weight.shape[0]
    blocks = order.shape[0]
    depth = width // blocks
    half = blocks // 2
    slots = 4

    def body(order_ref, gate_grad_ref, up_grad_ref, gate_ref, up_ref, own_out, other_out, held_ref, sems):
        def copies_of(n):
            at = pl.ds(pl.multiple_of(order_ref[n] * depth, depth), depth)
            return [
                pltpu.make_async_copy(source.at[at], held_ref.at[k, n % slots], sems.at[k, n % slots])
                for k, source in enumerate((gate_ref, up_ref))
            ]

        for n in range(slots - 1):
            for copy in copies_of(n):
                copy.start()
        for n in range(blocks):
            for copy in copies_of(n):
                copy.wait()
            if n + slots - 1 < blocks:
                for copy in copies_of(n + slots - 1):
                    copy.start()
            block = dot32(gate_grad_ref[...], held_ref[0, n % slots], contract_last) + dot32(
                up_grad_ref[...], held_ref[1, n % slots], contract_last
            )
            out = own_out if n < half else other_out
            out[n % half] = block.astype(jnp.bfloat16)

    return kernel_call(
        body,
        [in_smem, in_vmem, in_vmem, in_hbm, in_hbm],
        [shape_of((half, rows, depth))] * 2,
        18,
        [
            pltpu.VMEM((2, slots, depth, units), gate_weight.dtype),
            pltpu.SemaphoreType.DMA((2, slots)),
        ],
    )(order, gate_grad, up_grad, in_place(gate_weight), in_place(up_weight))


def weight_grads(input_columns, grads, gate_acts, up_acts):
    groups = len(grads)
    rows, units = grads[0].shape[0], gate_acts[0].shape[1]
    width = input_columns[0].shape[1]
    chunk = 256 if units % 256 == 0 else units
    chunks = units // chunk

    def body(*refs):
        columns, refs = refs[:groups], refs[groups:]
        (gate_out, up_out, turned, made, sems), refs = refs[3 * groups :], refs[: 3 * groups]
        turned[...] = jnp.concatenate([r[...] for r in columns], axis=0).T
        copies = []
        for i in range(chunks):
            at = pl.ds(i * chunk, chunk)
            hidden_grad, gate, up = (
                jnp.concatenate([r[:rows, at] for r in refs[k * groups : (k + 1) * groups]], axis=0)
                for k in range(3)
            )
            both = activation_grads(
                hidden_grad.astype(jnp.float32), gate.astype(jnp.float32), up.astype(jnp.float32)
            )
            for k, out in enumerate((gate_out, up_out)):
                made[k, i] = dot32(turned[...], both[k]).astype(jnp.bfloat16)
                copies.append(
                    pltpu.make_async_copy(made.at[k, i], out.at[:, at], sems.at[k, i])
                )
                copies[-1].start()
        for copy in copies:
            copy.wait()

    return pl.pallas_call(
        body,
        in_specs=[in_vmem] * (4 * groups),
        out_specs=[pl.BlockSpec(memory_space=pl.ANY)] * 2,
        out_shape=[shape_of((width, units))] * 2,
        scratch_shapes=[
            pltpu.VMEM((width, groups * rows), jnp.bfloat16),
            pltpu.VMEM((2, chunks, width, chunk), jnp.bfloat16),
            pltpu.SemaphoreType.DMA((2, chunks)),
        ],
        compiler_params=pltpu.CompilerParams(vmem_limit_bytes=18 * mib),
    )(*input_columns, *grads, *gate_acts, *up_acts)


def down_grads(grads, gate_acts, up_acts):
    groups = len(grads)
    rows, units = grads[0].shape[0], gate_acts[0].shape[1]
    width = grads[0].shape[1] - units
    chunk = 256 if units % 256 == 0 else units
    chunks = units // chunk

    def body(*refs):
        (out, made, sems), refs = refs[3 * groups :], refs[: 3 * groups]
        head_grad = jnp.concatenate([r[:, units:] for r in refs[:groups]], axis=0)
        copies = []
        for i in range(chunks):
            at = pl.ds(i * chunk, chunk)
            gate, up = (
                jnp.concatenate([r[:rows, at] for r in refs[k * groups : (k + 1) * groups]], axis=0)
                for k in (1, 2)
            )
            gate, up = gate.astype(jnp.float32), up.astype(jnp.float32)
            hidden = (gate * sigmoid(gate) * up).astype(jnp.bfloat16)
            made[i] = dot32(hidden, head_grad, contract_first).astype(jnp.bfloat16)
            copies.append(pltpu.make_async_copy(made.at[i], out.at[at], sems.at[i]))
            copies[-1].start()
        for copy in copies:
            copy.wait()

    return pl.pallas_call(
        body,
        in_specs=[in_vmem] * (3 * groups),
        out_specs=pl.BlockSpec(memory_space=pl.ANY),
        out_shape=shape_of((units, width)),
        scratch_shapes=[
            pltpu.VMEM((chunks, chunk, width), jnp.bfloat16),
            pltpu.SemaphoreType.DMA((chunks,)),
        ],
        compiler_params=pltpu.CompilerParams(vmem_limit_bytes=14 * mib),
    )(*grads, *gate_acts, *up_acts)


def shards(
    mlp_input,
    residual_in,
    gate_weight,
    up_weight,
    down_weight,
    span_index,
    positive_keys,
    request_rows,
    request_counts,
    negative_slots,
):
    dp_count = lax.axis_size("dp")
    fsdp_count = lax.axis_size("fsdp")
    chips = fsdp_count // 2
    place = jnp.stack([lax.axis_index("dp"), lax.axis_index("fsdp")])
    my_dp, my_fsdp = place[:1], place[1:]
    me = my_dp * fsdp_count + my_fsdp
    width = span_index.shape[1]
    own_queries = negative_slots.shape[0]
    group_rows = mlp_input.shape[0]
    j = jnp.arange(fsdp_count, dtype=jnp.int32)
    fsdp_order = jnp.bitwise_xor(my_fsdp, 2 * (j % chips) + j // chips).astype(jnp.int32)
    dp_order = jnp.bitwise_xor(my_dp, jnp.arange(dp_count, dtype=jnp.int32)).astype(jnp.int32)
    to_relative = relative_order(my_fsdp, fsdp_count, own_queries)
    j = jnp.arange(dp_count * chips, dtype=jnp.int32)
    asker = jnp.bitwise_xor(my_dp, j // chips) * fsdp_count + jnp.bitwise_xor(
        my_fsdp, 2 * (j % chips)
    )
    both = jnp.concatenate([me, jnp.bitwise_xor(me, 1)])
    place, fsdp_order, dp_order, to_relative, asker, both = together(
        place, fsdp_order, dp_order, to_relative, asker, both
    )

    slot_cap, negatives = request_rows.shape[2], negative_slots.shape[1]
    slots = jnp.concatenate([negative_slots // slot_cap, negative_slots % slot_cap], axis=1)
    slots = jnp.pad(slots, ((0, 0), (0, mlp_input.shape[1] - 2 * negatives)))
    message = jnp.concatenate([mlp_input, slots.astype(jnp.bfloat16)], axis=0)
    parts = forward_part(fsdp_order, message[None], (0,), group_rows, gate_weight, up_weight)
    first, *parts = together(gather_chips(message[None]), *parts)
    second = swap_core(first)
    gate_part, up_part = forward_part(
        fsdp_order, first, tuple(range(1, chips)), group_rows, gate_weight, up_weight, *parts
    )
    tables = jnp.concatenate([request_rows[:, 0, :], request_counts], axis=1)[None]
    gate_part, up_part, second, span_later, tables = together(
        gate_part, up_part, second, span_index, gather_core(tables)
    )
    units = up_weight.shape[1]
    bands = units // (2 * negatives)
    extra = [first[c, group_rows:, : 2 * negatives] for c in range(chips)]
    extra = [jnp.concatenate(extra[i : i + bands], axis=1) for i in range(0, chips, bands)]
    extra = [jnp.pad(x, ((0, 0), (0, units - x.shape[1]))) for x in extra]
    extra = jnp.concatenate(extra, axis=0)
    other_index = swap_core(span_later)
    gate_act, up_act, own_part, other_part = forward_rest(
        fsdp_order,
        second,
        gate_part,
        up_part,
        gate_weight,
        up_weight,
        down_weight,
        to_relative,
        extra,
    )

    near, far = 1, dp_count // 2
    own_part, other_part, other_index = together(own_part, other_part, other_index)
    own_part, received, gate_act, up_act, span_later, tables = together(
        own_part, swap_core(other_part), gate_act, up_act, span_later, tables
    )
    branch = add_up([own_part, received]).astype(jnp.bfloat16)

    tables = jnp.take(tables, asker, axis=1)
    row_tables, count_tables = tables[..., :-1], tables[..., -1:]
    top_state, gate_near, up_far, own_norm, span_later, other_index, row_tables, count_tables = together(
        sum_chips(branch) + residual_in.astype(jnp.float32),
        swap(gate_act, "dp", near),
        swap(up_act, "dp", far),
        norm_of(span_later.astype(jnp.float32)),
        span_later,
        other_index,
        row_tables,
        count_tables,
    )
    row_norm = norm_of(top_state)
    unit_rows = top_state / row_norm[:, None]

    states, last_slots, other_norm, span_later, other_index, row_tables, count_tables, positive_keys, both = together(
        gather_chips(top_state.astype(jnp.bfloat16)),
        swap(gate_near[group_rows:], "dp", far),
        swap_core(own_norm),
        span_later,
        other_index,
        row_tables,
        count_tables,
        positive_keys,
        both,
    )
    index_norm = jnp.concatenate([own_norm, other_norm], axis=0)
    slots = [x[group_rows:] for x in (gate_act, gate_near, up_far)] + [last_slots]
    slots = jnp.stack(slots).astype(jnp.int32)
    slots = [
        slots[
            :,
            c // bands * own_queries : (c // bands + 1) * own_queries,
            c % bands * 2 * negatives : (c % bands + 1) * 2 * negatives,
        ]
        for c in range(chips)
    ]
    slots = jnp.stack(slots, axis=1).reshape(dp_count * chips, own_queries, 2 * negatives)
    slots = slots[..., :negatives] * slot_cap + slots[..., negatives:]
    counts, dead = [], 0.0
    for k in range(2):
        shard_counts, shard_dead = use_counts(
            slots,
            row_tables[k],
            count_tables[k],
            both[k : k + 1],
            span_index.shape[0],
        )
        counts.append(shard_counts)
        dead = dead + shard_dead
    counts = jnp.concatenate(counts, axis=1)
    states = [states] + [swap(states, "dp", k) for k in range(1, dp_count)]
    counts, dead, *states = together(counts, dead, *states)
    index_parts = [span_later, other_index]
    pulls = score_kernel(
        states, index_parts, (1.0 / index_norm)[None, :], counts, dead[:, None], 128
    )

    sums = add_up([pulls[0]] + [swap(pulls[k], "dp", k) for k in range(1, dp_count)])
    sums, gate_act, up_act, first, second = together(
        sums.astype(jnp.bfloat16), gate_act, up_act, first, second
    )
    sums, gate_far, up_near, *blocks = together(
        sum_chips(sums),
        swap(gate_act, "dp", far),
        swap(up_act, "dp", near),
        *input_blocks(place, fsdp_order, first, second, group_rows, dp_count),
    )
    negative_total = sums[:, width]
    positive_rows = positive_keys.astype(jnp.float32)
    positive_unit = positive_rows / norm_of(positive_rows)[:, None]
    positive_score = inverse_temp * jnp.sum(unit_rows * positive_unit, axis=-1)
    exp_total = jnp.exp(positive_score) + negative_total
    query_loss = jnp.log(exp_total) - positive_score
    pull = (sums[:, :width] - negative_total[:, None] * positive_unit) / exp_total[:, None]
    inner = jnp.sum(pull * unit_rows, axis=-1)
    head_grad = (
        inverse_temp * (pull - inner[:, None] * unit_rows) / row_norm[:, None]
    ).astype(jnp.bfloat16)

    own_rows, block_near, block_far, gate_near, up_far = together(
        gather_chips(head_grad),
        swap(blocks[near], "dp", near),
        swap(blocks[far], "dp", far),
        gate_near,
        up_far,
    )
    gate_last, up_last = swap(gate_near, "dp", far), swap(up_far, "dp", near)
    other_rows = swap_core(own_rows)
    own_gate_grad, own_up_grad, grads = backward_hidden(
        dp_order, own_rows, other_rows, down_weight, gate_act, up_act, to_relative, dp_count
    )
    own_gate_grad, own_up_grad, gate_last, up_last, block_last, *grads = together(
        own_gate_grad,
        own_up_grad,
        gate_last,
        up_last,
        swap(blocks[near + far], "dp", near + far),
        *grads,
    )
    blocks = [blocks[0], block_near, block_far, block_last]
    gates = [gate_act, gate_near, gate_far, gate_last]
    ups = [up_act, up_near, up_far, up_last]
    grads = [grads[0]] + [swap(grads[k], "dp", k) for k in range(1, dp_count)]
    own_blocks, other_blocks = backward_input(
        fsdp_order, own_gate_grad, own_up_grad, gate_weight, up_weight
    )
    own_blocks, other_blocks, *grads = together(own_blocks, other_blocks, *grads)
    received = swap_core(other_blocks)
    down_grad = down_grads(grads, gates, ups)
    own_blocks, received, down_grad = together(own_blocks, received, down_grad)
    blocks_sum = add_up([own_blocks, received]).astype(jnp.bfloat16)
    input_grad = sum_chips(blocks_sum)[0].astype(jnp.bfloat16)
    gate_grad, up_grad = weight_grads(blocks, grads, gates, ups)
    return (query_loss, input_grad, gate_grad, up_grad, down_grad)


def solution(mesh):
    return jax.shard_map(
        shards,
        mesh=mesh,
        in_specs=(
            P("dp", "fsdp"),
            P(("dp", "fsdp"), None),
            P(None, "fsdp"),
            P(None, "fsdp"),
            P("fsdp", None),
            P(("dp", "fsdp"), None),
            P(("dp", "fsdp"), None),
            P(None, ("dp", "fsdp"), None),
            P(None, ("dp", "fsdp")),
            P(("dp", "fsdp"), None),
        ),
        out_specs=(
            P(("dp", "fsdp")),
            P("dp", "fsdp"),
            P("dp", "fsdp"),
            P("dp", "fsdp"),
            P("fsdp", "dp"),
        ),
        check_vma=False,
    )
```
